32 devices in a mesh: side: 2 (over y), grp: 8 (over z, x), tp: 2 (over core).
Axes of the slice: x: 2, y: 2, z: 4, core: 2. Of those that a mesh axis runs over, the one named last changes fastest.
Arguments:
- residual: bfloat16 [2, 128, 7168], P('side', 'grp'), may hold values from -14 to 14
- moe_gain: bfloat16 [2, 7168], P('side'), may hold values from 0.5 to 1.5
- router: bfloat16 [2, 16, 7168], P('side'), may hold values from -0.0625 to 0.0625
- routes: int32 [2, 128, 8], P('side', 'grp'), may hold values from 0 to 15, all different within a row; in each aligned block of 8 rows (0 to 7, 8 to 15, ..., all dimensions but the last counted through in order) at most 5 rows name the same one
- gate_w: bfloat16 [2, 7168, 16384], P('side', None, ('grp', 'tp')), may hold values from -0.0625 to 0.0625
- up_w: bfloat16 [2, 7168, 16384], P('side', None, ('grp', 'tp')), may hold values from -0.0625 to 0.0625
- down_w: bfloat16 [2, 16384, 7168], P('side', ('grp', 'tp')), may hold values from -0.1875 to 0.1875
- attn_gain: bfloat16 [2, 7168], P('side', 'tp'), may hold values from 0.5 to 1.5
- kv_proj: bfloat16 [2, 576, 7168], P('side', None, 'tp'), may hold values from -0.0625 to 0.0625
- kv_gain: bfloat16 [2, 512], P('side'), may hold values from 0.5 to 1.5
- cache_latent: bfloat16 [2, 128, 128, 512], P('side', 'grp'), may hold values from -5 to 5
- cache_rope: bfloat16 [2, 128, 64, 128], P('side', 'grp'), may hold values from -5 to 5
- lengths: int32 [2, 128], P('side', 'grp'), may hold values from 2 to 128, as said below
- query_latent: bfloat16 [2, 128, 64, 512], P('side', 'grp', 'tp'), may hold values from -34 to 34
- query_rope: bfloat16 [2, 128, 4096], P('side', 'grp', 'tp'), may hold values from -5 to 5
Outputs:
- resid_out: bfloat16 [2, 128, 7168], P('side', 'grp')
- new_latent: bfloat16 [2, 128, 512], P('side', 'grp')
- new_rope: bfloat16 [2, 128, 64], P('side', 'grp')
- attn_latent: bfloat16 [2, 128, 64, 512], P('side', 'grp', 'tp')
The draws below stay inside these ranges and needn't reach their ends.
Inputs may be any that keep to these rules, and one draw needn't show every extreme that they name: `routes`: within each aligned block of 8 rows every row names 8 different experts and no expert is named by more than 5 rows of the block. `lengths`: every attention group's 16 sequences include one with exactly 128 cached tokens.
All inputs are finite; a program needn't handle non-finite values.
Results may differ from the reference program's by a relative error of at most 0.015.
Values may be sent and summed in bfloat16 or wider, within the bound.
A program may use at most 128 MiB of HBM per device.

```python
import math
import jax
import jax.numpy as jnp
import numpy as np
from jax import lax

D = 7168
LAT = 512
ROPE = 64
HEADS = 64
FFW = 1024
EXPERTS = 16
TOP = 8
MB = 8
LMAX = 128
TOK = 16
TOKENS = 128
CAP = 5
KVW = 576
FF_DEV = 1024


def cache_core(key):
    return jax.random.normal(key, (2, TOKENS, LMAX, LAT), jnp.float32)


def draw_cache_latent(key, part):
    raw_draw = cache_core(key)
    return jnp.clip(raw_draw, -5.0, 5.0).astype(jnp.bfloat16)


def draw_query_latent(key, part):
    key = jax.random.fold_in(key, 5)
    first_key = jax.random.fold_in(key, 0)
    raw_draw = jax.random.normal(first_key, (2, TOKENS, HEADS, LAT), jnp.float32)
    return jnp.clip(raw_draw, -5.0, 5.0).astype(jnp.bfloat16)


def draw_residual(key, part):
    key = jax.random.fold_in(key, 1)
    first_key = jax.random.fold_in(key, 0)
    raw_draw = jax.random.normal(first_key, (2, TOKENS, D), jnp.float32)
    column_pos = jnp.arange(D, dtype=jnp.float32) / D
    rising = 3.0 ** column_pos
    return (0.6 * jnp.clip(raw_draw, -4.5, 4.5) * rising).astype(jnp.bfloat16)


def draw_lengths(key, part):
    key = jax.random.fold_in(key, 7)
    drawn_lengths = jax.random.randint(key, (2, TOKENS), 2, LMAX + 1, jnp.int32)
    positions = jnp.arange(TOKENS, dtype=jnp.int32)
    longest = positions % TOK == positions // TOK * 5 % TOK
    return jnp.where(longest[None, :], LMAX, drawn_lengths).astype(jnp.int32)


def block_levels(rng, dims, pieces, least, largest):
    def one(axis_at, blocks):
        steps = jax.random.uniform(jax.random.fold_in(jax.random.fold_in(rng, 6), axis_at), (blocks,), jnp.float32, least / len(pieces), largest / len(pieces))
        return jnp.repeat(jnp.exp(steps), dims[axis_at] // blocks).reshape((-1,) + (1,) * (len(dims) - axis_at - 1))

    level = one(*pieces[0])
    for cut in pieces[1:]:
        level = level * one(*cut)
    return level


def assign_block(key, own, number, rows, amount, top, most, slope):
    sequence = jax.random.permutation(key, amount)
    packed, common = shares(amount, rows * top, most, slope, True), shares(amount, rows * top, most, slope, False)
    places = jnp.arange(amount)

    def named(sizes, turn):
        used = int((sizes > 0).sum())
        fixed = max(1, used // 4)
        shifted = fixed + (places - fixed + turn * (used - fixed)) % max(1, amount - fixed)
        return jnp.zeros((amount,), jnp.int32).at[sequence[jnp.where(places < fixed, places, shifted)]].set(jnp.asarray(sizes, jnp.int32))

    sizes = jnp.where(number % 4 == 0, named(packed, number // 4), named(common, number - number // 4 - 1))
    mixed = jax.random.permutation(jax.random.fold_in(own, 3), amount)
    source_of, sink = mixed[0:amount // 2 * 2:2], mixed[1:amount // 2 * 2:2]
    room = jnp.minimum(sizes[source_of] - 1, most - sizes[sink]) // 2
    room = jnp.where((source_of == sequence[0]) | (sink == sequence[0]) | (sizes[sink] == 0), 0, jnp.maximum(room, 0))
    shifted = jax.random.randint(jax.random.fold_in(own, 4), (amount // 2,), 0, 1 << 20) % (room + 1)
    sizes = sizes.at[source_of].add(-shifted).at[sink].add(shifted)
    members = jnp.searchsorted(jnp.cumsum(sizes), jnp.arange(rows * top), side="right").astype(jnp.int32)
    grid = members.reshape(top, rows).T
    grid = grid[jax.random.permutation(jax.random.fold_in(own, 1), rows)]
    turn = jax.random.randint(jax.random.fold_in(own, 2), (rows, 1), 0, top)
    return jnp.take_along_axis(grid, (jnp.arange(top)[None, :] + turn) % top, axis=1)


def shares(number_of, total, limit, slope, full):
    portions = [(1 << 20) // math.isqrt(standing ** slope) + 1 for standing in range(1, number_of + 1)]
    largest = limit if full else min(limit, max(-(-total // number_of), total * portions[0] // sum(portions)))
    least = 1 if total - largest >= number_of - 1 else 0
    given, surplus = [largest] + [least] * (number_of - 1), total - largest - least * (number_of - 1)
    while surplus > 0:
        free = [i for i in range(1, number_of) if given[i] < largest] or [i for i in range(1, number_of) if given[i] < limit]
        mass, remaining = sum([portions[i] for i in free]), surplus
        for i in free:
            addition = min(limit - given[i], max(1, remaining * portions[i] // mass), surplus)
            given[i] = given[i] + addition
            surplus = surplus - addition
    return np.array(given)


def scatter_about(key, shape, scale, most, shards=(), kind=jnp.bfloat16):
    factor_of = block_levels(key, shape, shards, -0.22, 0.18) if shards else 1.0
    values = jax.random.normal(key, shape, jnp.float32) * scale * factor_of
    return jnp.minimum(jnp.maximum(values, -most), most).astype(kind)


def setup_inputs(seed: int = 0) -> dict:
    key_list = jax.random.split(jax.random.key(seed), 16)
    residual = draw_residual(jax.random.fold_in(key_list[15], 71), 0)
    moe_gain = jnp.clip(1.0 + 0.1 * jax.random.normal(key_list[1], (2, D), jnp.float32), 0.5, 1.5).astype(jnp.bfloat16)
    router = scatter_about(key_list[2], (2, EXPERTS, D), D ** -0.5, 0.0625, ((0, 2),))
    routes_keys = jax.random.split(jax.random.fold_in(key_list[3], 1), 2 * TOKENS // MB)
    routes_turns = jax.random.permutation(jax.random.fold_in(key_list[3], 3), 2 * TOKENS // MB)
    routes = jax.vmap(lambda own, number: assign_block(jax.random.fold_in(key_list[3], 2), own, number, MB, EXPERTS, TOP, CAP, 2))(routes_keys, routes_turns).reshape((2, TOKENS, TOP))
    gate_w = scatter_about(key_list[4], (2, D, EXPERTS * FFW), D ** -0.5, 0.0625, ((0, 2), (2, 16)))
    up_w = scatter_about(key_list[5], (2, D, EXPERTS * FFW), D ** -0.5, 0.0625, ((0, 2), (2, 16)))
    down_w = scatter_about(key_list[6], (2, EXPERTS * FFW, D), FFW ** -0.5, 0.1875, ((0, 2), (1, 16)))
    attn_gain = jnp.clip(1.0 + 0.1 * jax.random.normal(key_list[7], (2, D), jnp.float32), 0.5, 1.5).astype(jnp.bfloat16)
    kv_proj = scatter_about(key_list[8], (2, KVW, D), D ** -0.5, 0.0625, ((0, 2), (2, 2)))
    kv_gain = jnp.clip(1.0 + 0.1 * jax.random.normal(key_list[9], (2, LAT), jnp.float32), 0.5, 1.5).astype(jnp.bfloat16)
    cache_latent = draw_cache_latent(jax.random.fold_in(key_list[15], 71), 0)
    cache_rope = scatter_about(key_list[11], (2, TOKENS, ROPE, LMAX), 1.0, 5.0, ((0, 2), (1, 8)))
    lengths = draw_lengths(jax.random.fold_in(key_list[15], 71), 0)
    query_latent = draw_query_latent(jax.random.fold_in(key_list[15], 71), 0)
    query_rope = scatter_about(key_list[14], (2, TOKENS, HEADS * ROPE), 1.0, 5.0, ((0, 2), (1, 8), (2, 2)))
    return dict(residual=residual, moe_gain=moe_gain, router=router, routes=routes, gate_w=gate_w, up_w=up_w, down_w=down_w, attn_gain=attn_gain, kv_proj=kv_proj, kv_gain=kv_gain, cache_latent=cache_latent, cache_rope=cache_rope, lengths=lengths, query_latent=query_latent, query_rope=query_rope)


NORM_EPS = 1e-06
ROUTE_SCALE = 2.5
ROPE_BASE = 10000.0
SCORE_SCALE = 192.0 ** (-0.5)
FULL_PRECISION = lax.Precision.HIGHEST

def rms_scale(values):
    return lax.rsqrt(lax.optimization_barrier(jnp.mean(values * values, axis=-1, keepdims=True)) + NORM_EPS)

def rotate(pair_part, position):
    half_width = pair_part.shape[-1] // 2
    step_ids = lax.broadcasted_iota(jnp.int32, (1, half_width), 1).astype(jnp.float32)
    inverse_freq = jnp.exp(-(2.0 * step_ids / pair_part.shape[-1]) * jnp.log(ROPE_BASE))
    angles = position.astype(jnp.float32)[:, None] * inverse_freq
    first_half = pair_part[:, :half_width]
    second_half = pair_part[:, half_width:]
    cosine = jnp.cos(angles)
    sine_part = jnp.sin(angles)
    return jnp.concatenate([first_half * cosine - second_half * sine_part, first_half * sine_part + second_half * cosine], axis=-1)

def expert_outputs(row_block, gate_part, up_part, down_part):
    gate_val = jnp.dot(row_block, gate_part, preferred_element_type=jnp.float32)
    up_val = jnp.dot(row_block, up_part, preferred_element_type=jnp.float32)
    hidden = (jax.nn.silu(gate_val) * up_val).astype(jnp.bfloat16)
    running = jnp.zeros((row_block.shape[0], down_part.shape[1]), jnp.float32)
    for block_idx in range(FFW // FF_DEV):
        start = block_idx * FF_DEV
        piece_out = jnp.dot(hidden[:, start:start + FF_DEV], down_part[start:start + FF_DEV], preferred_element_type=jnp.float32).astype(jnp.bfloat16)
        running = running + lax.optimization_barrier(piece_out).astype(jnp.float32)
    return running

def reference(residual, moe_gain, router, routes, gate_w, up_w, down_w, attn_gain, kv_proj, kv_gain, cache_latent, cache_rope, lengths, query_latent, query_rope):
    x_rows = residual[0].astype(jnp.float32)
    normed = x_rows * rms_scale(x_rows) * moe_gain[0].astype(jnp.float32)
    logits = jnp.dot(normed, router[0].astype(jnp.float32).T, precision=FULL_PRECISION)
    moe_in = normed.astype(jnp.bfloat16)
    scores = jax.nn.sigmoid(logits)
    chosen = routes[0]
    picked = jnp.take_along_axis(scores, chosen, axis=1)
    weight = (ROUTE_SCALE * picked / lax.optimization_barrier(jnp.sum(picked, axis=1, keepdims=True))).astype(jnp.bfloat16)
    blocks = TOKENS // MB
    matches = (chosen[:, :, None] == jnp.arange(EXPERTS, dtype=jnp.int32)[None, None, :]).astype(jnp.int32)
    per_row = lax.optimization_barrier(jnp.sum(matches, axis=1)).astype(jnp.int32).reshape(blocks, MB, EXPERTS)
    before = (jnp.cumsum(per_row, axis=1).astype(jnp.int32) - per_row).reshape(TOKENS, EXPERTS)
    slots = lax.optimization_barrier(jnp.sum(matches * before[:, None, :], axis=2)).astype(jnp.int32)
    block_of = jnp.broadcast_to((jnp.arange(TOKENS, dtype=jnp.int32) // MB)[:, None], chosen.shape).astype(jnp.int32)
    values = jnp.broadcast_to(moe_in[:, None, :], (TOKENS, TOP, D))
    buffer = jnp.zeros((EXPERTS, blocks, CAP, D), jnp.bfloat16).at[chosen, block_of, slots].set(values)
    gate_all = gate_w[1].reshape(D, EXPERTS, FFW).transpose(1, 0, 2)
    up_all = up_w[1].reshape(D, EXPERTS, FFW).transpose(1, 0, 2)
    down_all = down_w[1].reshape(EXPERTS, FFW, D)

    def serve_expert(operands):
        row_block, gate_part, up_part, down_part = operands
        return expert_outputs(row_block.reshape(blocks * CAP, D), gate_part, up_part, down_part).reshape(blocks, CAP, D)
    served = lax.map(serve_expert, (buffer, gate_all, up_all, down_all))
    gathered = served[chosen, block_of, slots]
    moe_out = lax.optimization_barrier(jnp.sum(weight.astype(jnp.float32)[:, :, None] * gathered, axis=1))
    updated = (x_rows + moe_out).astype(jnp.bfloat16)
    updated_f = updated.astype(jnp.float32)
    scaled = (updated_f * attn_gain[0].astype(jnp.float32)).astype(jnp.bfloat16)
    kv_raw = jnp.dot(scaled, kv_proj[0].T, preferred_element_type=jnp.float32) * rms_scale(updated_f)
    latent = kv_raw[:, :LAT]
    fresh_lat = (latent * rms_scale(latent) * kv_gain[0].astype(jnp.float32)).astype(jnp.bfloat16)
    fresh_rot = rotate(kv_raw[:, LAT:], lengths[0]).astype(jnp.bfloat16)
    query_f = query_latent[0].astype(jnp.float32)
    query_r = query_rope[0].reshape(TOKENS, HEADS, ROPE).astype(jnp.float32)
    cache_f = cache_latent[0].astype(jnp.float32)
    cache_r = cache_rope[0].astype(jnp.float32)
    fresh_lat_f = fresh_lat.astype(jnp.float32)
    fresh_rot_f = fresh_rot.astype(jnp.float32)
    cache_scores = (jnp.einsum('thl,tpl->thp', query_f, cache_f, precision=FULL_PRECISION) + jnp.einsum('thr,trp->thp', query_r, cache_r, precision=FULL_PRECISION)) * SCORE_SCALE
    own_scores = (jnp.einsum('thl,tl->th', query_f, fresh_lat_f, precision=FULL_PRECISION) + jnp.einsum('thr,tr->th', query_r, fresh_rot_f, precision=FULL_PRECISION)) * SCORE_SCALE
    usable = jnp.arange(LMAX, dtype=jnp.int32)[None, None, :] < lengths[0][:, None, None]
    cache_scores = jnp.where(usable, cache_scores, -1e+30)
    peak = jnp.maximum(lax.optimization_barrier(jnp.max(cache_scores, axis=2)), own_scores)
    cache_weights = jnp.where(usable, jnp.exp(cache_scores - peak[:, :, None]), 0.0)
    own_weight = jnp.exp(own_scores - peak)
    denominator = lax.optimization_barrier(jnp.sum(cache_weights, axis=2)) + own_weight
    cache_probs = (cache_weights / denominator[:, :, None]).astype(jnp.bfloat16)
    own_probs = (own_weight / denominator).astype(jnp.bfloat16)
    mixed = jnp.einsum('thp,tpl->thl', cache_probs.astype(jnp.float32), cache_f, precision=FULL_PRECISION)
    mixed = mixed + own_probs.astype(jnp.float32)[:, :, None] * fresh_lat_f[:, None, :]
    attended = mixed.astype(jnp.bfloat16)
    return (jnp.stack([updated, jnp.zeros_like(updated)]), jnp.stack([fresh_lat, jnp.zeros_like(fresh_lat)]), jnp.stack([fresh_rot, jnp.zeros_like(fresh_rot)]), jnp.stack([attended, jnp.zeros_like(attended)]))
```

```python
import functools
import math

import jax
import jax.numpy as jnp
from jax import lax
from jax.experimental import pallas as pl
from jax.experimental.pallas import tpu as pltpu
from jax.sharding import PartitionSpec as P

NORM_EPS = 1e-06
ROUTE_SCALE = 2.5
ROPE_BASE = 10000.0
SCORE_SCALE = 192.0 ** (-0.5)
MESH = pl.DeviceIdType.MESH
CHUNKS = 4
NT = (((1,), (1,)), ((), ()))


def kernel(
    n_grp, n_tp, res_ref, gain_ref, router_ref, routes_ref, again_ref, kvgain_ref, len_ref,
    qrope_ref, gate_ref, up_ref, down_ref, kvp_ref, cache_ref, crope_ref, qlat_ref,
    resid_ref, nlat_ref, nrope_ref, attn_ref,
    msg, xb, wg, wu, wd, acc_g, acc_u, hid, pown, pother, r0, sx, r1, tbuf, ra, hs, hr,
    kvs, kvr, kvw, cl, cr, ql, o_acc, m_acc, l_acc,
    load_sem, d_send, d_recv, f_send, x_send, x_recv, c_send, c_recv, z_send, z_recv, h_send, h_recv, k_sem,
):
    side = lax.axis_index("side")
    grp = lax.axis_index("grp")
    tp = lax.axis_index("tp")
    n_a = n_grp // 2
    a = grp // 2
    b = grp % 2
    rows, width = res_ref.shape
    half = width // 2
    cw = half // CHUNKS
    experts = router_ref.shape[0]
    ff = gate_ref.shape[2]
    lat = kvgain_ref.shape[1]
    rope = crope_ref.shape[2]
    kvwid = lat + rope
    core_peer = (side, grp, 1 - tp)
    x_peer = (side, a * 2 + 1 - b, tp)

    def line(other_side, where):
        return (other_side, where * 2 + b, tp)

    def remote(src, dst, ssem, rsem, dev):
        return pltpu.make_async_remote_copy(
            src_ref=src, dst_ref=dst, send_sem=ssem, recv_sem=rsem, device_id=dev, device_id_type=MESH
        )

    def block(ref, which, pos):
        return ref.at[which, pl.ds(pl.multiple_of(pos * rows, rows), rows), :]

    barrier = pltpu.get_barrier_semaphore()

    def greet():
        pl.semaphore_signal(barrier, inc=1, device_id=core_peer, device_id_type=MESH)
        for i in range(n_a):
            pl.semaphore_signal(barrier, inc=1, device_id=line(1 - side, i), device_id_type=MESH)

    @pl.when(side == 1)
    def _():
        own = pl.multiple_of(tp * half, 128)
        oth = pl.multiple_of((1 - tp) * half, 128)
        loads = []
        for i, at in enumerate((own, oth)):
            loads.append(pltpu.make_async_copy(gate_ref.at[0, pl.ds(at, half), :], wg.at[i], load_sem.at[i]))
            loads.append(pltpu.make_async_copy(up_ref.at[0, pl.ds(at, half), :], wu.at[i], load_sem.at[2 + i]))
        for i, at in enumerate((own, oth)):
            loads.append(pltpu.make_async_copy(down_ref.at[0, :, pl.ds(at, half)], wd.at[i], load_sem.at[4 + i]))
        for ld in loads:
            ld.start()
        greet()
        pl.semaphore_signal(barrier, inc=1, device_id=x_peer, device_id_type=MESH)
        pl.semaphore_wait(barrier, n_a + 2)

        sends = []
        for d in range(n_a):
            src_a = lax.rem(a - d + n_a, n_a)
            pos = b * n_a + src_a
            here = block(xb, 0, pos)
            remote(here, here, f_send.at[0, d], d_recv.at[0, pos], core_peer).wait_recv()
            fwd = remote(here, here, x_send.at[d], d_recv.at[0, pos], x_peer)
            fwd.start()
            cfwd = remote(here, block(xb, 1, pos), f_send.at[0, d], d_recv.at[1, pos], core_peer)
            cfwd.start()
            sends += [fwd, cfwd]
        for d in range(n_a):
            src_a = lax.rem(a - d + n_a, n_a)
            pos = (1 - b) * n_a + src_a
            here = block(xb, 0, pos)
            remote(here, here, f_send.at[1, d], d_recv.at[0, pos], core_peer).wait_recv()
            cfwd = remote(here, block(xb, 1, pos), f_send.at[1, d], d_recv.at[1, pos], core_peer)
            cfwd.start()
            sends.append(cfwd)

        tn = min(256, ff)
        loads[0].wait()
        loads[1].wait()

        @pl.loop(0, ff // tn)
        def _(n):
            cols = pl.ds(pl.multiple_of(n * tn, tn), tn)
            x0 = xb[0, :, :half]
            acc_g[:, cols] = jnp.dot(x0, wg[0, :, cols], preferred_element_type=jnp.float32)
            acc_u[:, cols] = jnp.dot(x0, wu[0, :, cols], preferred_element_type=jnp.float32)

        for pos in range(n_grp):
            here = block(xb, 1, pos)
            remote(here, here, f_send.at[0, 0], d_recv.at[1, pos], core_peer).wait_recv()
        loads[2].wait()
        loads[3].wait()

        @pl.loop(0, ff // tn)
        def _(n):
            cols = pl.ds(pl.multiple_of(n * tn, tn), tn)
            x1 = xb[1, :, :half]
            g = acc_g[:, cols] + jnp.dot(x1, wg[1, :, cols], preferred_element_type=jnp.float32)
            u = acc_u[:, cols] + jnp.dot(x1, wu[1, :, cols], preferred_element_type=jnp.float32)
            hid[:, cols] = (g / (1.0 + jnp.exp(-g)) * u).astype(jnp.bfloat16)

        loads[4].wait()
        loads[5].wait()
        span = n_grp * n_tp // experts
        expert = (grp * n_tp + tp) // span
        table = xb[0, :, half:].astype(jnp.float32)
        lanes = lax.broadcasted_iota(jnp.int32, table.shape, 1)
        weight = jnp.sum(jnp.where(lanes == expert, table, 0.0), axis=1, keepdims=True)
        half_rows = n_a * rows
        mine = pl.ds(pl.multiple_of(b * half_rows, rows), half_rows)
        theirs = pl.ds(pl.multiple_of((1 - b) * half_rows, rows), half_rows)

        def down(j):
            h = hid[...]
            cols = slice(j * cw, (j + 1) * cw)
            p1 = jnp.dot(h, wd[1, :, cols], preferred_element_type=jnp.float32)
            pother[j] = (p1 * weight).astype(jnp.bfloat16)
            cp = remote(pother.at[j], r0.at[j], c_send.at[j], c_recv.at[j], core_peer)
            cp.start()
            p0 = jnp.dot(h, wd[0, :, cols], preferred_element_type=jnp.float32)
            pown[j] = (p0 * weight).astype(jnp.bfloat16)
            return cp

        def stage_x(j, cp):
            cp.wait_recv()
            sx[j] = (pown[j, theirs, :].astype(jnp.float32) + r0[j, theirs, :].astype(jnp.float32)).astype(jnp.bfloat16)
            xp = remote(sx.at[j], r1.at[j], x_send.at[n_a + j], x_recv.at[j], x_peer)
            xp.start()
            return xp

        def stage_z(j, xp):
            xp.wait_recv()
            tbuf[j] = (
                pown[j, mine, :].astype(jnp.float32)
                + r0[j, mine, :].astype(jnp.float32)
                + r1[j].astype(jnp.float32)
            ).astype(jnp.bfloat16)
            out = []
            for d in range(n_a):
                to_a = lax.rem(a + d, n_a)
                zp = remote(
                    block(tbuf, j, to_a), ra.at[j, a], z_send.at[j, d], z_recv.at[j, a], line(0, to_a)
                )
                zp.start()
                out.append(zp)
            return out

        cps, xps = [], []
        for j in range(CHUNKS):
            cps.append(down(j))
            if j >= 1:
                xps.append(stage_x(j - 1, cps[j - 1]))
        xps.append(stage_x(CHUNKS - 1, cps[-1]))
        for j in range(CHUNKS):
            sends += stage_z(j, xps[j])
        resid_ref[...] = jnp.zeros_like(resid_ref)
        nlat_ref[...] = jnp.zeros_like(nlat_ref)
        nrope_ref[...] = jnp.zeros_like(nrope_ref)
        attn_ref[...] = jnp.zeros_like(attn_ref)
        for cp in sends + cps + xps:
            cp.wait_send()

    @pl.when(side == 0)
    def _():
        loads = [
            pltpu.make_async_copy(qlat_ref.at[0], ql, load_sem.at[0]),
            pltpu.make_async_copy(cache_ref.at[0], cl, load_sem.at[1]),
            pltpu.make_async_copy(crope_ref.at[0], cr, load_sem.at[2]),
            pltpu.make_async_copy(kvp_ref.at[0], kvw, load_sem.at[3]),
        ]
        for ld in loads:
            ld.start()
        greet()
        x = res_ref[...].astype(jnp.float32)
        scale = lax.rsqrt(jnp.mean(x * x, axis=1, keepdims=True) + NORM_EPS)
        normed = x * scale * gain_ref[...].astype(jnp.float32)
        logits = lax.dot_general(
            normed, router_ref[...].astype(jnp.float32), NT,
            precision=lax.Precision.HIGHEST, preferred_element_type=jnp.float32,
        )
        s = 1.0 / (1.0 + jnp.exp(-logits))
        ids = lax.broadcasted_iota(jnp.int32, s.shape, 1)
        chosen = jnp.zeros(s.shape, jnp.float32)
        for k in range(routes_ref.shape[1]):
            chosen = jnp.where(routes_ref[:, k : k + 1] == ids, 1.0, chosen)
        picked = s * chosen
        dense = ROUTE_SCALE * picked / jnp.sum(picked, axis=1, keepdims=True)
        narrow = normed.astype(jnp.bfloat16)
        msg[:, :half] = jnp.where(tp == 0, narrow[:, :half], narrow[:, half:])
        msg[:, half:] = jnp.zeros((rows, 128), jnp.bfloat16)
        msg[:, half : half + experts] = dense.astype(jnp.bfloat16)
        pl.semaphore_wait(barrier, n_a + 1)
        pos = b * n_a + a
        sends = []
        for d in range(n_a):
            to_a = lax.rem(a + d, n_a)
            cp = remote(msg, block(xb, 0, pos), d_send.at[d], d_recv.at[0, pos], line(1, to_a))
            cp.start()
            sends.append(cp)

        for ld in loads:
            ld.wait()

        @pl.loop(0, rows)
        def _(t):
            sc = lax.dot_general(ql[t], cl[t], NT, preferred_element_type=jnp.float32)
            sc = sc + jnp.dot(qrope_ref[t], cr[t], preferred_element_type=jnp.float32)
            sc = sc * SCORE_SCALE
            usable = lax.broadcasted_iota(jnp.int32, sc.shape, 1) < len_ref[t]
            sc = jnp.where(usable, sc, -1e30)
            peak = jnp.max(sc, axis=1, keepdims=True)
            wts = jnp.where(usable, jnp.exp(sc - peak), 0.0)
            m_acc[t] = jnp.broadcast_to(peak, sc.shape)
            l_acc[t] = jnp.broadcast_to(jnp.sum(wts, axis=1, keepdims=True), sc.shape)
            o_acc[t] = jnp.dot(wts.astype(jnp.bfloat16), cl[t], preferred_element_type=jnp.float32)

        kv = jnp.zeros((rows, kvwid), jnp.float32)
        sq = jnp.zeros((rows, 1), jnp.float32)
        for j in range(CHUNKS):
            total = jnp.zeros((rows, cw), jnp.float32)
            for i in range(n_a):
                here = ra.at[j, i]
                remote(here, here, h_send.at[j], z_recv.at[j, i], core_peer).wait_recv()
                total = total + ra[j, i].astype(jnp.float32)
            cols = pl.ds(pl.multiple_of(tp * half + j * cw, 128), cw)
            h = (res_ref[:, cols].astype(jnp.float32) + total).astype(jnp.bfloat16)
            hs[j] = h
            cp = remote(hs.at[j], hr.at[j], h_send.at[j], h_recv.at[j], core_peer)
            cp.start()
            sends.append(cp)
            resid_ref[:, cols] = h
            hf = h.astype(jnp.float32)
            span = slice(j * cw, (j + 1) * cw)
            scaled = (hf * again_ref[:, span].astype(jnp.float32)).astype(jnp.bfloat16)
            kv = kv + lax.dot_general(scaled, kvw[:, span], NT, preferred_element_type=jnp.float32)
            sq = sq + jnp.sum(hf * hf, axis=1, keepdims=True)
        kvs[:, :kvwid] = kv
        kvs[:, kvwid:] = jnp.broadcast_to(sq, (rows, kvs.shape[1] - kvwid))
        cp = remote(kvs, kvr, k_sem.at[0], k_sem.at[1], core_peer)
        cp.start()
        sends.append(cp)
        cp.wait_recv()
        both = kvs[...] + kvr[...]
        norm = lax.rsqrt(both[:, kvwid : kvwid + 1] / width + NORM_EPS)
        latent = both[:, :lat] * norm
        lscale = lax.rsqrt(jnp.mean(latent * latent, axis=1, keepdims=True) + NORM_EPS)
        fresh = (latent * lscale * kvgain_ref[...].astype(jnp.float32)).astype(jnp.bfloat16)
        nlat_ref[...] = fresh
        rot = both[:, lat:] * norm
        lane = lax.broadcasted_iota(jnp.int32, rot.shape, 1)
        step = jnp.where(lane < rope // 2, lane, lane - rope // 2).astype(jnp.float32)
        freq = jnp.exp(-(2.0 * step / rope) * math.log(ROPE_BASE))
        row_id = lax.broadcasted_iota(jnp.int32, rot.shape, 0)
        position = jnp.zeros(rot.shape, jnp.float32)
        for t in range(rows):
            position = jnp.where(row_id == t, len_ref[t].astype(jnp.float32), position)
        angle = position * freq
        up_part = pltpu.roll(rot, 128 - rope // 2, 1)
        down_part = pltpu.roll(rot, rope // 2, 1)
        turned = rot * jnp.cos(angle) + jnp.where(lane < rope // 2, -up_part, down_part) * jnp.sin(angle)
        turned = turned[:, :rope].astype(jnp.bfloat16)
        nrope_ref[...] = turned
        fresh_f = fresh.astype(jnp.float32)
        turned_f = turned.astype(jnp.float32)
        for t in range(rows):
            fl = fresh_f[t : t + 1]
            own = jnp.sum(ql[t].astype(jnp.float32) * fl, axis=1, keepdims=True)
            own = own + jnp.sum(qrope_ref[t].astype(jnp.float32) * turned_f[t : t + 1], axis=1, keepdims=True)
            own = own * SCORE_SCALE
            m_old = m_acc[t, :, :1]
            peak = jnp.maximum(m_old, own)
            keep = jnp.exp(m_old - peak)
            ow = jnp.exp(own - peak)
            inv = 1.0 / (l_acc[t, :, :1] * keep + ow)
            attn_ref[t] = (o_acc[t] * (keep * inv) + (ow * inv) * fl).astype(jnp.bfloat16)
        for j in range(CHUNKS):
            here = hr.at[j]
            remote(here, here, h_send.at[j], h_recv.at[j], core_peer).wait_recv()
            cols = pl.ds(pl.multiple_of((1 - tp) * half + j * cw, 128), cw)
            resid_ref[:, cols] = hr[j]
        for cp in sends:
            cp.wait_send()


def body(
    residual, moe_gain, router, routes, gate_w, up_w, down_w, attn_gain, kv_proj, kv_gain,
    cache_latent, cache_rope, lengths, query_latent, query_rope,
):
    n_grp = lax.axis_size("grp")
    n_tp = lax.axis_size("tp")
    n_a = n_grp // 2
    rows, width = residual.shape[1:]
    half = width // 2
    cw = half // CHUNKS
    ff = gate_w.shape[2]
    all_rows = n_grp * rows
    lat = kv_gain.shape[1]
    heads = query_latent.shape[2]
    slots = cache_latent.shape[2]
    rope = cache_rope.shape[2]
    bf, f32 = jnp.bfloat16, jnp.float32
    vmem, smem, hbm = (pl.BlockSpec(memory_space=s) for s in (pltpu.VMEM, pltpu.SMEM, pl.ANY))
    dma = pltpu.SemaphoreType.DMA
    q_rot = query_rope[0].reshape(rows, heads, rope)
    outs = pl.pallas_call(
        functools.partial(kernel, n_grp, n_tp),
        out_shape=(
            jax.ShapeDtypeStruct((rows, width), bf),
            jax.ShapeDtypeStruct((rows, lat), bf),
            jax.ShapeDtypeStruct((rows, rope), bf),
            jax.ShapeDtypeStruct((rows, heads, lat), bf),
        ),
        in_specs=[vmem] * 6 + [smem, vmem] + [hbm] * 7,
        out_specs=(vmem,) * 4,
        scratch_shapes=[
            pltpu.VMEM((rows, half + 128), bf),
            pltpu.VMEM((2, all_rows, half + 128), bf),
            pltpu.VMEM((2, half, ff), bf),
            pltpu.VMEM((2, half, ff), bf),
            pltpu.VMEM((2, ff, half), bf),
            pltpu.VMEM((all_rows, ff), f32),
            pltpu.VMEM((all_rows, ff), f32),
            pltpu.VMEM((all_rows, ff), bf),
            pltpu.VMEM((CHUNKS, all_rows, cw), bf),
            pltpu.VMEM((CHUNKS, all_rows, cw), bf),
            pltpu.VMEM((CHUNKS, all_rows, cw), bf),
            pltpu.VMEM((CHUNKS, n_a * rows, cw), bf),
            pltpu.VMEM((CHUNKS, n_a * rows, cw), bf),
            pltpu.VMEM((CHUNKS, n_a * rows, cw), bf),
            pltpu.VMEM((CHUNKS, n_a, rows, cw), bf),
            pltpu.VMEM((CHUNKS, rows, cw), bf),
            pltpu.VMEM((CHUNKS, rows, cw), bf),
            pltpu.VMEM((rows, lat + 128), f32),
            pltpu.VMEM((rows, lat + 128), f32),
            pltpu.VMEM(kv_proj.shape[1:], bf),
            pltpu.VMEM(cache_latent.shape[1:], bf),
            pltpu.VMEM(cache_rope.shape[1:], bf),
            pltpu.VMEM(query_latent.shape[1:], bf),
            pltpu.VMEM((rows, heads, lat), f32),
            pltpu.VMEM((rows, heads, slots), f32),
            pltpu.VMEM((rows, heads, slots), f32),
            dma((6,)),
            dma((n_a,)),
            dma((2, n_grp)),
            dma((2, n_a)),
            dma((n_a + CHUNKS,)),
            dma((CHUNKS,)),
            dma((CHUNKS,)),
            dma((CHUNKS,)),
            dma((CHUNKS, n_a)),
            dma((CHUNKS, n_a)),
            dma((CHUNKS,)),
            dma((CHUNKS,)),
            dma((2,)),
        ],
        compiler_params=pltpu.CompilerParams(
            collective_id=0, has_side_effects=True, vmem_limit_bytes=63 * 1024 * 1024
        ),
    )(
        residual[0], moe_gain, router[0], routes[0], attn_gain, kv_gain, lengths[0], q_rot,
        gate_w, up_w, down_w, kv_proj, cache_latent, cache_rope, query_latent,
    )
    return tuple(o[None] for o in outs)


def solution(mesh):
    in_specs = (
        P("side", "grp", None),
        P("side", None),
        P("side", None, None),
        P("side", "grp", None),
        P("side", None, ("grp", "tp")),
        P("side", None, ("grp", "tp")),
        P("side", ("grp", "tp"), None),
        P("side", "tp"),
        P("side", None, "tp"),
        P("side", None),
        P("side", "grp", None, None),
        P("side", "grp", None, None),
        P("side", "grp"),
        P("side", "grp", "tp", None),
        P("side", "grp", "tp"),
    )
    out_specs = (
        P("side", "grp", None),
        P("side", "grp", None),
        P("side", "grp", None),
        P("side", "grp", "tp", None),
    )
    return jax.shard_map(body, mesh=mesh, in_specs=in_specs, out_specs=out_specs, check_vma=False)
```

```python
import functools
import math

import jax
import jax.numpy as jnp
from jax import lax
from jax.experimental import pallas as pl
from jax.experimental.pallas import tpu as pltpu
from jax.sharding import PartitionSpec as P

NORM_EPS = 1e-06
ROUTE_SCALE = 2.5
ROPE_BASE = 10000.0
SCORE_SCALE = 192.0 ** (-0.5)
MESH = pl.DeviceIdType.MESH
CHUNKS = 7
PIECES = 4
NT = (((1,), (1,)), ((), ()))


def kernel(
    n_grp, n_tp, res_ref, gain_ref, router_ref, routes_ref, again_ref, kvgain_ref, len_ref,
    qrope_ref, gate_ref, up_ref, down_ref, kvp_ref, cache_ref, crope_ref, qlat_ref,
    resid_ref, nlat_ref, nrope_ref, attn_ref,
    msg, xb, wg, wu, wd, acc_g, acc_u, hid, pown, pother, r0, sx, r1, tbuf, ra, hs, hr,
    kvs, kvr, kvw, cl, cr, qr, ql, o_acc, m_acc, l_acc,
    load_sem, d_send, d_recv, f_send, f_recv, x_send, y_send, x_recv, c_send, c_recv, z_send, z_recv, h_send, h_recv, k_sem,
):
    side = lax.axis_index("side")
    grp = lax.axis_index("grp")
    tp = lax.axis_index("tp")
    n_a = n_grp // 2
    a = grp // 2
    b = grp % 2
    rows, width = res_ref.shape
    half = width // 2
    cw = half // CHUNKS
    kc = half // PIECES
    experts = router_ref.shape[0]
    ff = gate_ref.shape[2]
    lat = kvgain_ref.shape[1]
    rope = crope_ref.shape[2]
    kvwid = lat + rope
    core_peer = (side, grp, 1 - tp)
    x_peer = (side, a * 2 + 1 - b, tp)

    def line(other_side, where):
        return (other_side, where * 2 + b, tp)

    def remote(src, dst, ssem, rsem, dev):
        return pltpu.make_async_remote_copy(
            src_ref=src, dst_ref=dst, send_sem=ssem, recv_sem=rsem, device_id=dev, device_id_type=MESH
        )

    def block(ref, which, k, pos):
        at = pl.ds(pl.multiple_of(pos * rows, rows), rows)
        return ref.at[which, k, at, :] if k == PIECES - 1 else ref.at[which, k, at, :kc]

    barrier = pltpu.get_barrier_semaphore()

    def greet():
        pl.semaphore_signal(barrier, inc=1, device_id=core_peer, device_id_type=MESH)
        for i in range(n_a):
            pl.semaphore_signal(barrier, inc=1, device_id=line(1 - side, i), device_id_type=MESH)

    @pl.when(side == 1)
    def _():
        own = pl.multiple_of(tp * half, 128)
        oth = pl.multiple_of((1 - tp) * half, 128)
        loads = []
        for k in range(PIECES):
            piece = pl.ds(k * kc, kc)
            for i, at in enumerate((own, oth)):
                source = pl.ds(pl.multiple_of(at + k * kc, 128), kc)
                for w_ref, w_vmem in ((gate_ref, wg), (up_ref, wu)):
                    loads.append(
                        pltpu.make_async_copy(
                            w_ref.at[0, source, :], w_vmem.at[i, piece, :], load_sem.at[len(loads)]
                        )
                    )
        for i, at in enumerate((own, oth)):
            loads.append(
                pltpu.make_async_copy(down_ref.at[0, :, pl.ds(at, half)], wd.at[i], load_sem.at[len(loads)])
            )
        for ld in loads:
            ld.start()
        greet()
        pl.semaphore_signal(barrier, inc=1, device_id=x_peer, device_id_type=MESH)
        pl.semaphore_wait(barrier, n_a + 2)

        sends = []

        def direct(k):
            for d in range(n_a):
                pos = b * n_a + lax.rem(a - d + n_a, n_a)
                here = block(xb, 0, k, pos)
                remote(here, here, f_send.at[k], d_recv.at[k, pos], core_peer).wait_recv()
                fwd = remote(here, here, x_send.at[k, d], d_recv.at[k, pos], x_peer)
                fwd.start()
                sends.append(fwd)

        def across(k):
            for d in range(n_a):
                pos = (1 - b) * n_a + lax.rem(a - d + n_a, n_a)
                here = block(xb, 0, k, pos)
                remote(here, here, f_send.at[k], d_recv.at[k, pos], core_peer).wait_recv()
            cp = remote(xb.at[0, k, :, :kc], xb.at[1, k, :, :kc], f_send.at[k], f_recv.at[k], core_peer)
            cp.start()
            sends.append(cp)
            return cp

        tn = min(256, ff)

        def products(k, cp):
            cp.wait_recv()
            for ld in loads[4 * k : 4 * k + 4]:
                ld.wait()
            span_k = slice(k * kc, (k + 1) * kc)

            @pl.loop(0, ff // tn)
            def _(n):
                cols = pl.ds(pl.multiple_of(n * tn, tn), tn)
                x0 = xb[0, k, :, :kc]
                x1 = xb[1, k, :, :kc]
                g = jnp.dot(x0, wg[0, span_k, cols], preferred_element_type=jnp.float32)
                g = g + jnp.dot(x1, wg[1, span_k, cols], preferred_element_type=jnp.float32)
                u = jnp.dot(x0, wu[0, span_k, cols], preferred_element_type=jnp.float32)
                u = u + jnp.dot(x1, wu[1, span_k, cols], preferred_element_type=jnp.float32)
                if k > 0:
                    g = g + acc_g[:, cols]
                    u = u + acc_u[:, cols]
                if k < PIECES - 1:
                    acc_g[:, cols] = g
                    acc_u[:, cols] = u
                else:
                    hid[:, cols] = (g / (1.0 + jnp.exp(-g)) * u).astype(jnp.bfloat16)

        direct(0)
        for k in range(1, PIECES):
            direct(k)
            products(k - 1, across(k - 1))
        products(PIECES - 1, across(PIECES - 1))

        loads[-2].wait()
        loads[-1].wait()
        span = n_grp * n_tp // experts
        expert = (grp * n_tp + tp) // span
        table = xb[0, PIECES - 1, :, kc:].astype(jnp.float32)
        lanes = lax.broadcasted_iota(jnp.int32, table.shape, 1)
        weight = jnp.sum(jnp.where(lanes == expert, table, 0.0), axis=1, keepdims=True)
        half_rows = n_a * rows
        mine = pl.ds(pl.multiple_of(b * half_rows, rows), half_rows)
        theirs = pl.ds(pl.multiple_of((1 - b) * half_rows, rows), half_rows)

        def down(j):
            h = hid[...]
            cols = slice(j * cw, (j + 1) * cw)
            p1 = jnp.dot(h, wd[1, :, cols], preferred_element_type=jnp.float32)
            pother[j] = (p1 * weight).astype(jnp.bfloat16)
            cp = remote(pother.at[j], r0.at[j], c_send.at[j], c_recv.at[j], core_peer)
            cp.start()
            p0 = jnp.dot(h, wd[0, :, cols], preferred_element_type=jnp.float32)
            pown[j] = (p0 * weight).astype(jnp.bfloat16)
            return cp

        def stage_x(j, cp):
            cp.wait_recv()
            sx[j] = (pown[j, theirs, :].astype(jnp.float32) + r0[j, theirs, :].astype(jnp.float32)).astype(jnp.bfloat16)
            xp = remote(sx.at[j], r1.at[j], y_send.at[j], x_recv.at[j], x_peer)
            xp.start()
            return xp

        def stage_z(j, xp):
            xp.wait_recv()
            tbuf[j] = (
                pown[j, mine, :].astype(jnp.float32)
                + r0[j, mine, :].astype(jnp.float32)
                + r1[j].astype(jnp.float32)
            ).astype(jnp.bfloat16)
            out = []
            for d in range(n_a):
                to_a = lax.rem(a + d, n_a)
                zp = remote(
                    tbuf.at[j, pl.ds(pl.multiple_of(to_a * rows, rows), rows), :], ra.at[j, a], z_send.at[j, d], z_recv.at[j, a], line(0, to_a)
                )
                zp.start()
                out.append(zp)
            return out

        cps, xps = [], []
        for j in range(CHUNKS):
            cps.append(down(j))
            if j >= 1:
                xps.append(stage_x(j - 1, cps[j - 1]))
        xps.append(stage_x(CHUNKS - 1, cps[-1]))
        for j in range(CHUNKS):
            sends += stage_z(j, xps[j])
        resid_ref[...] = jnp.zeros_like(resid_ref)
        nlat_ref[...] = jnp.zeros_like(nlat_ref)
        nrope_ref[...] = jnp.zeros_like(nrope_ref)
        attn_ref[...] = jnp.zeros_like(attn_ref)
        for cp in sends + cps + xps:
            cp.wait_send()

    @pl.when(side == 0)
    def _():
        loads = [
            pltpu.make_async_copy(qlat_ref.at[0], ql, load_sem.at[0]),
            pltpu.make_async_copy(cache_ref.at[0], cl, load_sem.at[1]),
            pltpu.make_async_copy(crope_ref.at[0], cr.at[:, :rope, :], load_sem.at[2]),
            pltpu.make_async_copy(crope_ref.at[0], cr.at[:, rope:, :], load_sem.at[3]),
            pltpu.make_async_copy(kvp_ref.at[0], kvw, load_sem.at[4]),
        ]
        for ld in loads:
            ld.start()
        greet()
        x = res_ref[...].astype(jnp.float32)
        scale = lax.rsqrt(jnp.mean(x * x, axis=1, keepdims=True) + NORM_EPS)
        pos = b * n_a + a
        sends = []

        def dispatch(k):
            for d in range(n_a):
                to_a = lax.rem(a + d, n_a)
                piece = msg.at[k] if k == PIECES - 1 else msg.at[k, :, :kc]
                cp = remote(piece, block(xb, 0, k, pos), d_send.at[k, d], d_recv.at[k, pos], line(1, to_a))
                cp.start()
                sends.append(cp)

        for k in range(PIECES):
            cols = pl.ds(pl.multiple_of(tp * half + k * kc, 128), kc)
            part = res_ref[:, cols].astype(jnp.float32) * scale * gain_ref[:, cols].astype(jnp.float32)
            msg[k, :, :kc] = part.astype(jnp.bfloat16)
        pl.semaphore_wait(barrier, n_a + 1)
        for k in range(PIECES - 1):
            dispatch(k)
        normed = x * scale * gain_ref[...].astype(jnp.float32)
        logits = lax.dot_general(
            router_ref[...].astype(jnp.float32), normed, NT,
            precision=lax.Precision.HIGHEST, preferred_element_type=jnp.float32,
        )
        s = 1.0 / (1.0 + jnp.exp(-logits))
        ids = lax.broadcasted_iota(jnp.int32, s.shape, 0)
        chosen = jnp.zeros(s.shape, jnp.float32)
        for k in range(routes_ref.shape[0]):
            chosen = jnp.where(routes_ref[k : k + 1, :] == ids, 1.0, chosen)
        picked = s * chosen
        dense = (ROUTE_SCALE * picked / jnp.sum(picked, axis=0, keepdims=True)).astype(jnp.bfloat16)
        eye_r = lax.broadcasted_iota(jnp.int32, (rows, rows), 0)
        eye_c = lax.broadcasted_iota(jnp.int32, (rows, rows), 1)
        eye = jnp.where(eye_r == eye_c, 1.0, 0.0).astype(jnp.bfloat16)
        dense = lax.dot_general(eye, dense, NT, preferred_element_type=jnp.float32)
        msg[PIECES - 1, :, kc:] = jnp.zeros((rows, 128), jnp.bfloat16)
        msg[PIECES - 1, :, kc : kc + experts] = dense.astype(jnp.bfloat16)
        dispatch(PIECES - 1)

        for ld in loads:
            ld.wait()

        heads = ql.shape[1]
        head_id = lax.broadcasted_iota(jnp.int32, (heads, 2 * rope), 0)
        lane_id = lax.broadcasted_iota(jnp.int32, (heads, 2 * rope), 1)
        for t in range(rows):
            fold = jnp.zeros((heads, 2 * rope), jnp.float32)
            for i in range(heads // 2):
                pair = qrope_ref[t : t + 1, i * 2 * rope : (i + 1) * 2 * rope].astype(jnp.float32)
                owner = jnp.where(lane_id < rope, 2 * i, 2 * i + 1)
                fold = jnp.where(head_id == owner, pair, fold)
            qr[t] = fold.astype(jnp.bfloat16)

        @pl.loop(0, rows)
        def _(t):
            sc = lax.dot_general(ql[t], cl[t], NT, preferred_element_type=jnp.float32)
            sc = sc + jnp.dot(qr[t], cr[t], preferred_element_type=jnp.float32)
            sc = sc * SCORE_SCALE
            usable = lax.broadcasted_iota(jnp.int32, sc.shape, 1) < len_ref[t]
            sc = jnp.where(usable, sc, -1e30)
            peak = jnp.max(sc, axis=1, keepdims=True)
            wts = jnp.where(usable, jnp.exp(sc - peak), 0.0)
            m_acc[t] = jnp.broadcast_to(peak, sc.shape)
            l_acc[t] = jnp.broadcast_to(jnp.sum(wts, axis=1, keepdims=True), sc.shape)
            o_acc[t] = jnp.dot(wts.astype(jnp.bfloat16), cl[t], preferred_element_type=jnp.float32)

        wide = (rows, 2 * rope)
        lane = lax.broadcasted_iota(jnp.int32, wide, 1)
        step = (lane % (rope // 2)).astype(jnp.float32)
        freq = jnp.exp(-(2.0 * step / rope) * math.log(ROPE_BASE))
        row_id = lax.broadcasted_iota(jnp.int32, wide, 0)
        position = jnp.zeros(wide, jnp.float32)
        for t in range(rows):
            position = jnp.where(row_id == t, len_ref[t].astype(jnp.float32), position)
        angle = position * freq
        cosine = jnp.cos(angle)
        sine = jnp.where(lane < rope // 2, -jnp.sin(angle), jnp.sin(angle))
        kv = jnp.zeros((rows, kvwid), jnp.float32)
        sq = jnp.zeros((rows, 1), jnp.float32)
        for j in range(CHUNKS):
            total = jnp.zeros((rows, cw), jnp.float32)
            for i in range(n_a):
                here = ra.at[j, i]
                remote(here, here, h_send.at[j], z_recv.at[j, i], core_peer).wait_recv()
                total = total + ra[j, i].astype(jnp.float32)
            cols = pl.ds(pl.multiple_of(tp * half + j * cw, 128), cw)
            h = (res_ref[:, cols].astype(jnp.float32) + total).astype(jnp.bfloat16)
            hs[j] = h
            cp = remote(hs.at[j], hr.at[j], h_send.at[j], h_recv.at[j], core_peer)
            cp.start()
            sends.append(cp)
            resid_ref[:, cols] = h
            hf = h.astype(jnp.float32)
            span = slice(j * cw, (j + 1) * cw)
            scaled = (hf * again_ref[:, span].astype(jnp.float32)).astype(jnp.bfloat16)
            kv = kv + lax.dot_general(scaled, kvw[:, span], NT, preferred_element_type=jnp.float32)
            sq = sq + jnp.sum(hf * hf, axis=1, keepdims=True)
        kvs[:, :kvwid] = kv
        kvs[:, kvwid:] = jnp.broadcast_to(sq, (rows, kvs.shape[1] - kvwid))
        cp = remote(kvs, kvr, k_sem.at[0], k_sem.at[1], core_peer)
        cp.start()
        sends.append(cp)
        cp.wait_recv()
        both = kvs[...] + kvr[...]
        norm = lax.rsqrt(both[:, kvwid : kvwid + 1] / width + NORM_EPS)
        latent = both[:, :lat] * norm
        lscale = lax.rsqrt(jnp.mean(latent * latent, axis=1, keepdims=True) + NORM_EPS)
        fresh = (latent * lscale * kvgain_ref[...].astype(jnp.float32)).astype(jnp.bfloat16)
        nlat_ref[...] = fresh
        rot = both[:, lat:] * norm
        up_part = pltpu.roll(rot, 128 - rope // 2, 1)
        down_part = pltpu.roll(rot, rope // 2, 1)
        turned = rot * cosine + jnp.where(lane < rope // 2, up_part, down_part) * sine
        nrope_ref[...] = turned[:, :rope].astype(jnp.bfloat16)
        turned = jnp.where(lane < rope, turned, pltpu.roll(turned, rope, 1)).astype(jnp.bfloat16)
        fresh_f = fresh.astype(jnp.float32)
        turned_f = turned.astype(jnp.float32)
        for t in range(rows):
            fl = fresh_f[t : t + 1]
            own = jnp.sum(ql[t].astype(jnp.float32) * fl, axis=1, keepdims=True)
            own = own + jnp.sum(qr[t].astype(jnp.float32) * turned_f[t : t + 1], axis=1, keepdims=True)
            own = own * SCORE_SCALE
            m_old = m_acc[t, :, :1]
            peak = jnp.maximum(m_old, own)
            keep = jnp.exp(m_old - peak)
            ow = jnp.exp(own - peak)
            inv = 1.0 / (l_acc[t, :, :1] * keep + ow)
            attn_ref[t] = (o_acc[t] * (keep * inv) + (ow * inv) * fl).astype(jnp.bfloat16)
        for j in range(CHUNKS):
            here = hr.at[j]
            remote(here, here, h_send.at[j], h_recv.at[j], core_peer).wait_recv()
            cols = pl.ds(pl.multiple_of((1 - tp) * half + j * cw, 128), cw)
            resid_ref[:, cols] = hr[j]
        for cp in sends:
            cp.wait_send()


def hand_over(*refs):
    sem = refs[-1]
    copies = [pltpu.make_async_copy(refs[i], refs[4 + i], sem.at[i]) for i in range(4)]
    for cp in copies:
        cp.start()
    for cp in copies:
        cp.wait()


def body(
    residual, moe_gain, router, routes, gate_w, up_w, down_w, attn_gain, kv_proj, kv_gain,
    cache_latent, cache_rope, lengths, query_latent, query_rope,
):
    n_grp = lax.axis_size("grp")
    n_tp = lax.axis_size("tp")
    n_a = n_grp // 2
    rows, width = residual.shape[1:]
    half = width // 2
    cw = half // CHUNKS
    kc = half // PIECES
    ff = gate_w.shape[2]
    all_rows = n_grp * rows
    lat = kv_gain.shape[1]
    heads = query_latent.shape[2]
    slots = cache_latent.shape[2]
    rope = cache_rope.shape[2]
    bf, f32 = jnp.bfloat16, jnp.float32
    vmem, smem, hbm = (pl.BlockSpec(memory_space=s) for s in (pltpu.VMEM, pltpu.SMEM, pl.ANY))
    dma = pltpu.SemaphoreType.DMA
    outs = pl.pallas_call(
        functools.partial(kernel, n_grp, n_tp),
        out_shape=(
            jax.ShapeDtypeStruct((rows, width), bf),
            jax.ShapeDtypeStruct((rows, lat), bf),
            jax.ShapeDtypeStruct((rows, rope), bf),
            jax.ShapeDtypeStruct((rows, heads, lat), bf),
        ),
        in_specs=[vmem] * 6 + [smem, vmem] + [hbm] * 7,
        out_specs=(vmem,) * 4,
        scratch_shapes=[
            pltpu.VMEM((PIECES, rows, kc + 128), bf),
            pltpu.VMEM((2, PIECES, all_rows, kc + 128), bf),
            pltpu.VMEM((2, half, ff), bf),
            pltpu.VMEM((2, half, ff), bf),
            pltpu.VMEM((2, ff, half), bf),
            pltpu.VMEM((all_rows, ff), f32),
            pltpu.VMEM((all_rows, ff), f32),
            pltpu.VMEM((all_rows, ff), bf),
            pltpu.VMEM((CHUNKS, all_rows, cw), bf),
            pltpu.VMEM((CHUNKS, all_rows, cw), bf),
            pltpu.VMEM((CHUNKS, all_rows, cw), bf),
            pltpu.VMEM((CHUNKS, n_a * rows, cw), bf),
            pltpu.VMEM((CHUNKS, n_a * rows, cw), bf),
            pltpu.VMEM((CHUNKS, n_a * rows, cw), bf),
            pltpu.VMEM((CHUNKS, n_a, rows, cw), bf),
            pltpu.VMEM((CHUNKS, rows, cw), bf),
            pltpu.VMEM((CHUNKS, rows, cw), bf),
            pltpu.VMEM((rows, lat + 128), f32),
            pltpu.VMEM((rows, lat + 128), f32),
            pltpu.VMEM(kv_proj.shape[1:], bf),
            pltpu.VMEM(cache_latent.shape[1:], bf),
            pltpu.VMEM((rows, 2 * rope, slots), bf),
            pltpu.VMEM((rows, heads, 2 * rope), bf),
            pltpu.VMEM(query_latent.shape[1:], bf),
            pltpu.VMEM((rows, heads, lat), f32),
            pltpu.VMEM((rows, heads, slots), f32),
            pltpu.VMEM((rows, heads, slots), f32),
            dma((4 * PIECES + 2,)),
            dma((PIECES, n_a)),
            dma((PIECES, n_grp)),
            dma((PIECES,)),
            dma((PIECES,)),
            dma((PIECES, n_a)),
            dma((CHUNKS,)),
            dma((CHUNKS,)),
            dma((CHUNKS,)),
            dma((CHUNKS,)),
            dma((CHUNKS, n_a)),
            dma((CHUNKS, n_a)),
            dma((CHUNKS,)),
            dma((CHUNKS,)),
            dma((2,)),
        ],
        compiler_params=pltpu.CompilerParams(
            collective_id=0, has_side_effects=True, vmem_limit_bytes=63 * 1024 * 1024
        ),
    )(
        residual[0], moe_gain, router[0], routes[0].T, attn_gain, kv_gain, lengths[0], query_rope[0],
        gate_w, up_w, down_w, kv_proj, cache_latent, cache_rope, query_latent,
    )
    final = pl.pallas_call(
        hand_over,
        out_shape=tuple(jax.ShapeDtypeStruct(o.shape, bf) for o in outs),
        in_specs=[hbm] * 4,
        out_specs=(hbm,) * 4,
        scratch_shapes=[dma((4,))],
        compiler_params=pltpu.CompilerParams(vmem_limit_bytes=63 * 1024 * 1024),
    )(*outs)
    return tuple(o[None] for o in final)


def solution(mesh):
    in_specs = (
        P("side", "grp", None),
        P("side", None),
        P("side", None, None),
        P("side", "grp", None),
        P("side", None, ("grp", "tp")),
        P("side", None, ("grp", "tp")),
        P("side", ("grp", "tp"), None),
        P("side", "tp"),
        P("side", None, "tp"),
        P("side", None),
        P("side", "grp", None, None),
        P("side", "grp", None, None),
        P("side", "grp"),
        P("side", "grp", "tp", None),
        P("side", "grp", "tp"),
    )
    out_specs = (
        P("side", "grp", None),
        P("side", "grp", None),
        P("side", "grp", None),
        P("side", "grp", "tp", None),
    )
    return jax.shard_map(body, mesh=mesh, in_specs=in_specs, out_specs=out_specs, check_vma=False)
```

```python
import functools
import math

import jax
import jax.numpy as jnp
from jax import lax
from jax.experimental import pallas as pl
from jax.experimental.pallas import tpu as pltpu
from jax.sharding import PartitionSpec as P

NORM_EPS = 1e-06
ROUTE_SCALE = 2.5
ROPE_BASE = 10000.0
SCORE_SCALE = 192.0 ** (-0.5)
MESH = pl.DeviceIdType.MESH
CHUNKS = 7
PIECES = 7
NT = (((1,), (1,)), ((), ()))


def kernel(
    n_grp, n_tp, res_ref, gain_ref, router_ref, routes_ref, again_ref, kvgain_ref, len_ref,
    qrope_ref, gate_ref, up_ref, down_ref, kvp_ref, cache_ref, crope_ref, qlat_ref,
    resid_ref, nlat_ref, nrope_ref, attn_ref,
    msg, xb, wg, wu, wd, acc_g, acc_u, hid, pown, pother, r0, sx, r1, tbuf, ra, hs, hr,
    kvs, kvr, kvw, cl, cr, qr, ql, o_acc, m_acc, l_acc,
    load_sem, d_send, d_recv, f_send, f_recv, x_send, y_send, x_recv, c_send, c_recv, z_send, z_recv, h_send, h_recv, k_sem,
):
    side = lax.axis_index("side")
    grp = lax.axis_index("grp")
    tp = lax.axis_index("tp")
    n_a = n_grp // 2
    a = grp // 2
    b = grp % 2
    rows, width = res_ref.shape
    half = width // 2
    cw = half // CHUNKS
    kc = half // PIECES
    experts = router_ref.shape[0]
    ff = gate_ref.shape[2]
    lat = kvgain_ref.shape[1]
    rope = crope_ref.shape[2]
    kvwid = lat + rope
    core_peer = (side, grp, 1 - tp)
    x_peer = (side, a * 2 + 1 - b, tp)

    def line(other_side, where):
        return (other_side, where * 2 + b, tp)

    def remote(src, dst, ssem, rsem, dev):
        return pltpu.make_async_remote_copy(
            src_ref=src, dst_ref=dst, send_sem=ssem, recv_sem=rsem, device_id=dev, device_id_type=MESH
        )

    def block(ref, which, k, pos):
        at = pl.ds(pl.multiple_of(pos * rows, rows), rows)
        return ref.at[which, k, at, :] if k == PIECES - 1 else ref.at[which, k, at, :kc]

    barrier = pltpu.get_barrier_semaphore()

    def greet():
        pl.semaphore_signal(barrier, inc=1, device_id=core_peer, device_id_type=MESH)
        for i in range(n_a):
            pl.semaphore_signal(barrier, inc=1, device_id=line(1 - side, i), device_id_type=MESH)

    @pl.when(side == 1)
    def _():
        greet()
        pl.semaphore_signal(barrier, inc=1, device_id=x_peer, device_id_type=MESH)
        own = pl.multiple_of(tp * half, 128)
        oth = pl.multiple_of((1 - tp) * half, 128)
        loads = []
        for k in range(PIECES):
            piece = pl.ds(k * kc, kc)
            for i, at in enumerate((own, oth)):
                source = pl.ds(pl.multiple_of(at + k * kc, 128), kc)
                for w_ref, w_vmem in ((gate_ref, wg), (up_ref, wu)):
                    loads.append(
                        pltpu.make_async_copy(
                            w_ref.at[0, source, :], w_vmem.at[i, piece, :], load_sem.at[len(loads)]
                        )
                    )
        for i, at in enumerate((own, oth)):
            loads.append(
                pltpu.make_async_copy(down_ref.at[0, :, pl.ds(at, half)], wd.at[i], load_sem.at[len(loads)])
            )
        for ld in loads:
            ld.start()
        pl.semaphore_wait(barrier, n_a + 2)

        sends = []

        def direct(k):
            for d in range(n_a):
                pos = b * n_a + lax.rem(a - d + n_a, n_a)
                here = block(xb, 0, k, pos)
                remote(here, here, f_send.at[k], d_recv.at[k, pos], core_peer).wait_recv()
                fwd = remote(here, here, x_send.at[k, d], d_recv.at[k, pos], x_peer)
                fwd.start()
                sends.append(fwd)

        def across(k):
            for d in range(n_a):
                pos = (1 - b) * n_a + lax.rem(a - d + n_a, n_a)
                here = block(xb, 0, k, pos)
                remote(here, here, f_send.at[k], d_recv.at[k, pos], core_peer).wait_recv()
            cp = remote(xb.at[0, k, :, :kc], xb.at[1, k, :, :kc], f_send.at[k], f_recv.at[k], core_peer)
            cp.start()
            sends.append(cp)
            return cp

        tn = min(512, ff)

        def products(k, i):
            loads[4 * k + 2 * i].wait()
            loads[4 * k + 2 * i + 1].wait()
            span_k = slice(k * kc, (k + 1) * kc)

            @pl.loop(0, ff // tn)
            def _(n):
                cols = pl.ds(pl.multiple_of(n * tn, tn), tn)
                xk = xb[i, k, :, :kc]
                g = jnp.dot(xk, wg[i, span_k, cols], preferred_element_type=jnp.float32)
                u = jnp.dot(xk, wu[i, span_k, cols], preferred_element_type=jnp.float32)
                if k + i > 0:
                    g = g + acc_g[:, cols]
                    u = u + acc_u[:, cols]
                if k + i < PIECES:
                    acc_g[:, cols] = g
                    acc_u[:, cols] = u
                else:
                    hid[:, cols] = (g / (1.0 + jnp.exp(-g)) * u).astype(jnp.bfloat16)

        direct(0)
        for k in range(PIECES):
            cp = across(k)
            if 0 < k < PIECES - 1:
                direct(k + 1)
            products(k, 0)
            if k == 0:
                direct(1)
            cp.wait_recv()
            products(k, 1)

        loads[-2].wait()
        loads[-1].wait()
        span = n_grp * n_tp // experts
        expert = (grp * n_tp + tp) // span
        table = xb[0, PIECES - 1, :, kc:].astype(jnp.float32)
        lanes = lax.broadcasted_iota(jnp.int32, table.shape, 1)
        weight = jnp.sum(jnp.where(lanes == expert, table, 0.0), axis=1, keepdims=True)
        half_rows = n_a * rows
        mine = pl.ds(pl.multiple_of(b * half_rows, rows), half_rows)
        theirs = pl.ds(pl.multiple_of((1 - b) * half_rows, rows), half_rows)

        def down(j):
            h = hid[...]
            cols = slice(j * cw, (j + 1) * cw)
            p1 = jnp.dot(h, wd[1, :, cols], preferred_element_type=jnp.float32)
            pother[j] = (p1 * weight).astype(jnp.bfloat16)
            cp = remote(pother.at[j], r0.at[j], c_send.at[j], c_recv.at[j], core_peer)
            cp.start()
            p0 = jnp.dot(h, wd[0, :, cols], preferred_element_type=jnp.float32)
            pown[j] = (p0 * weight).astype(jnp.bfloat16)
            return cp

        def stage_x(j, cp):
            cp.wait_recv()
            sx[j] = (pown[j, theirs, :].astype(jnp.float32) + r0[j, theirs, :].astype(jnp.float32)).astype(jnp.bfloat16)
            xp = remote(sx.at[j], r1.at[j], y_send.at[j], x_recv.at[j], x_peer)
            xp.start()
            return xp

        def stage_z(j, xp):
            xp.wait_recv()
            tbuf[j] = (
                pown[j, mine, :].astype(jnp.float32)
                + r0[j, mine, :].astype(jnp.float32)
                + r1[j].astype(jnp.float32)
            ).astype(jnp.bfloat16)
            out = []
            for d in range(n_a):
                to_a = lax.rem(a + d, n_a)
                zp = remote(
                    tbuf.at[j, pl.ds(pl.multiple_of(to_a * rows, rows), rows), :], ra.at[j, a], z_send.at[j, d], z_recv.at[j, a], line(0, to_a)
                )
                zp.start()
                out.append(zp)
            return out

        cps, xps = [], []
        for j in range(CHUNKS):
            cps.append(down(j))
            if j >= 1:
                xps.append(stage_x(j - 1, cps[j - 1]))
        xps.append(stage_x(CHUNKS - 1, cps[-1]))
        for j in range(CHUNKS):
            sends += stage_z(j, xps[j])
        resid_ref[...] = jnp.zeros_like(resid_ref)
        nlat_ref[...] = jnp.zeros_like(nlat_ref)
        nrope_ref[...] = jnp.zeros_like(nrope_ref)
        attn_ref[...] = jnp.zeros_like(attn_ref)
        for cp in sends + cps + xps:
            cp.wait_send()

    @pl.when(side == 0)
    def _():
        loads = [
            pltpu.make_async_copy(qlat_ref.at[0], ql, load_sem.at[0]),
            pltpu.make_async_copy(cache_ref.at[0], cl, load_sem.at[1]),
            pltpu.make_async_copy(crope_ref.at[0], cr.at[:, :rope, :], load_sem.at[2]),
            pltpu.make_async_copy(crope_ref.at[0], cr.at[:, rope:, :], load_sem.at[3]),
            pltpu.make_async_copy(kvp_ref.at[0], kvw, load_sem.at[4]),
        ]
        greet()
        for ld in loads:
            ld.start()
        x = res_ref[...].astype(jnp.float32)
        scale = lax.rsqrt(jnp.mean(x * x, axis=1, keepdims=True) + NORM_EPS)
        pos = b * n_a + a
        sends = []

        def dispatch(k):
            for d in range(n_a):
                to_a = lax.rem(a + d, n_a)
                piece = msg.at[k] if k == PIECES - 1 else msg.at[k, :, :kc]
                cp = remote(piece, block(xb, 0, k, pos), d_send.at[k, d], d_recv.at[k, pos], line(1, to_a))
                cp.start()
                sends.append(cp)

        for k in range(PIECES):
            cols = pl.ds(pl.multiple_of(tp * half + k * kc, 128), kc)
            part = res_ref[:, cols].astype(jnp.float32) * scale * gain_ref[:, cols].astype(jnp.float32)
            msg[k, :, :kc] = part.astype(jnp.bfloat16)
        pl.semaphore_wait(barrier, n_a + 1)
        for k in range(PIECES - 1):
            dispatch(k)
        normed = x * scale * gain_ref[...].astype(jnp.float32)
        logits = lax.dot_general(
            router_ref[...].astype(jnp.float32), normed, NT,
            precision=lax.Precision.HIGHEST, preferred_element_type=jnp.float32,
        )
        s = 1.0 / (1.0 + jnp.exp(-logits))
        ids = lax.broadcasted_iota(jnp.int32, s.shape, 0)
        chosen = jnp.zeros(s.shape, jnp.float32)
        for k in range(routes_ref.shape[0]):
            chosen = jnp.where(routes_ref[k : k + 1, :] == ids, 1.0, chosen)
        picked = s * chosen
        dense = (ROUTE_SCALE * picked / jnp.sum(picked, axis=0, keepdims=True)).astype(jnp.bfloat16)
        eye_r = lax.broadcasted_iota(jnp.int32, (rows, rows), 0)
        eye_c = lax.broadcasted_iota(jnp.int32, (rows, rows), 1)
        eye = jnp.where(eye_r == eye_c, 1.0, 0.0).astype(jnp.bfloat16)
        dense = lax.dot_general(eye, dense, NT, preferred_element_type=jnp.float32)
        msg[PIECES - 1, :, kc:] = jnp.zeros((rows, 128), jnp.bfloat16)
        msg[PIECES - 1, :, kc : kc + experts] = dense.astype(jnp.bfloat16)
        dispatch(PIECES - 1)

        for ld in loads:
            ld.wait()

        heads = ql.shape[1]
        head_id = lax.broadcasted_iota(jnp.int32, (heads, 2 * rope), 0)
        lane_id = lax.broadcasted_iota(jnp.int32, (heads, 2 * rope), 1)
        for t in range(rows):
            fold = jnp.zeros((heads, 2 * rope), jnp.float32)
            for i in range(heads // 2):
                pair = qrope_ref[t : t + 1, i * 2 * rope : (i + 1) * 2 * rope].astype(jnp.float32)
                owner = jnp.where(lane_id < rope, 2 * i, 2 * i + 1)
                fold = jnp.where(head_id == owner, pair, fold)
            qr[t] = fold.astype(jnp.bfloat16)

        @pl.loop(0, rows)
        def _(t):
            sc = lax.dot_general(ql[t], cl[t], NT, preferred_element_type=jnp.float32)
            sc = sc + jnp.dot(qr[t], cr[t], preferred_element_type=jnp.float32)
            sc = sc * SCORE_SCALE
            usable = lax.broadcasted_iota(jnp.int32, sc.shape, 1) < len_ref[t]
            sc = jnp.where(usable, sc, -1e30)
            peak = jnp.max(sc, axis=1, keepdims=True)
            wts = jnp.where(usable, jnp.exp(sc - peak), 0.0)
            m_acc[t] = jnp.broadcast_to(peak, sc.shape)
            l_acc[t] = jnp.broadcast_to(jnp.sum(wts, axis=1, keepdims=True), sc.shape)
            o_acc[t] = jnp.dot(wts.astype(jnp.bfloat16), cl[t], preferred_element_type=jnp.float32)

        wide = (rows, 2 * rope)
        lane = lax.broadcasted_iota(jnp.int32, wide, 1)
        step = (lane % (rope // 2)).astype(jnp.float32)
        freq = jnp.exp(-(2.0 * step / rope) * math.log(ROPE_BASE))
        row_id = lax.broadcasted_iota(jnp.int32, wide, 0)
        position = jnp.zeros(wide, jnp.float32)
        for t in range(rows):
            position = jnp.where(row_id == t, len_ref[t].astype(jnp.float32), position)
        angle = position * freq
        cosine = jnp.cos(angle)
        sine = jnp.where(lane < rope // 2, -jnp.sin(angle), jnp.sin(angle))
        kv = jnp.zeros((rows, kvwid), jnp.float32)
        sq = jnp.zeros((rows, 1), jnp.float32)
        for j in range(CHUNKS):
            total = jnp.zeros((rows, cw), jnp.float32)
            for i in range(n_a):
                here = ra.at[j, i]
                remote(here, here, h_send.at[j], z_recv.at[j, i], core_peer).wait_recv()
                total = total + ra[j, i].astype(jnp.float32)
            cols = pl.ds(pl.multiple_of(tp * half + j * cw, 128), cw)
            h = (res_ref[:, cols].astype(jnp.float32) + total).astype(jnp.bfloat16)
            hs[j] = h
            cp = remote(hs.at[j], hr.at[j], h_send.at[j], h_recv.at[j], core_peer)
            cp.start()
            sends.append(cp)
            resid_ref[:, cols] = h
            hf = h.astype(jnp.float32)
            span = slice(j * cw, (j + 1) * cw)
            scaled = (hf * again_ref[:, span].astype(jnp.float32)).astype(jnp.bfloat16)
            kv = kv + lax.dot_general(scaled, kvw[:, span], NT, preferred_element_type=jnp.float32)
            sq = sq + jnp.sum(hf * hf, axis=1, keepdims=True)
        kvs[:, :kvwid] = kv
        kvs[:, kvwid:] = jnp.broadcast_to(sq, (rows, kvs.shape[1] - kvwid))
        cp = remote(kvs, kvr, k_sem.at[0], k_sem.at[1], core_peer)
        cp.start()
        sends.append(cp)
        cp.wait_recv()
        both = kvs[...] + kvr[...]
        norm = lax.rsqrt(both[:, kvwid : kvwid + 1] / width + NORM_EPS)
        latent = both[:, :lat] * norm
        lscale = lax.rsqrt(jnp.mean(latent * latent, axis=1, keepdims=True) + NORM_EPS)
        fresh = (latent * lscale * kvgain_ref[...].astype(jnp.float32)).astype(jnp.bfloat16)
        nlat_ref[...] = fresh
        rot = both[:, lat:] * norm
        up_part = pltpu.roll(rot, 128 - rope // 2, 1)
        down_part = pltpu.roll(rot, rope // 2, 1)
        turned = rot * cosine + jnp.where(lane < rope // 2, up_part, down_part) * sine
        nrope_ref[...] = turned[:, :rope].astype(jnp.bfloat16)
        turned = jnp.where(lane < rope, turned, pltpu.roll(turned, rope, 1)).astype(jnp.bfloat16)
        fresh_f = fresh.astype(jnp.float32)
        flat = rows * heads
        own = lax.dot_general(ql[...].reshape(flat, lat), fresh, NT, preferred_element_type=jnp.float32)
        own = own + lax.dot_general(
            qr[...].reshape(flat, 2 * rope), turned, NT, preferred_element_type=jnp.float32
        )
        own_row = lax.broadcasted_iota(jnp.int32, own.shape, 0) // heads
        own_col = lax.broadcasted_iota(jnp.int32, own.shape, 1)
        own = jnp.sum(jnp.where(own_row == own_col, own, 0.0), axis=1, keepdims=True) * SCORE_SCALE
        m_old = m_acc[...].reshape(flat, m_acc.shape[2])[:, :1]
        l_old = l_acc[...].reshape(flat, l_acc.shape[2])[:, :1]
        peak = jnp.maximum(m_old, own)
        keep = jnp.exp(m_old - peak)
        ow = jnp.exp(own - peak)
        inv = 1.0 / (l_old * keep + ow)
        keep = keep * inv
        ow = ow * inv
        for t in range(rows):
            at = slice(t * heads, (t + 1) * heads)
            attn_ref[t] = (o_acc[t] * keep[at] + ow[at] * fresh_f[t : t + 1]).astype(jnp.bfloat16)
        for j in range(CHUNKS):
            here = hr.at[j]
            remote(here, here, h_send.at[j], h_recv.at[j], core_peer).wait_recv()
            cols = pl.ds(pl.multiple_of((1 - tp) * half + j * cw, 128), cw)
            resid_ref[:, cols] = hr[j]
        for cp in sends:
            cp.wait_send()


def hand_over(*refs):
    ins, outs, held, sem = refs[:4], refs[4:8], refs[8:12], refs[12]
    first = [pltpu.make_async_copy(ins[i], held[i], sem.at[0, i]) for i in range(4)]
    second = [pltpu.make_async_copy(held[i], outs[i], sem.at[1, i]) for i in range(4)]
    for cp in first:
        cp.start()
    for into, out in zip(first, second):
        into.wait()
        out.start()
    for cp in second:
        cp.wait()


def body(
    residual, moe_gain, router, routes, gate_w, up_w, down_w, attn_gain, kv_proj, kv_gain,
    cache_latent, cache_rope, lengths, query_latent, query_rope,
):
    n_grp = lax.axis_size("grp")
    n_tp = lax.axis_size("tp")
    n_a = n_grp // 2
    rows, width = residual.shape[1:]
    half = width // 2
    cw = half // CHUNKS
    kc = half // PIECES
    ff = gate_w.shape[2]
    all_rows = n_grp * rows
    lat = kv_gain.shape[1]
    heads = query_latent.shape[2]
    slots = cache_latent.shape[2]
    rope = cache_rope.shape[2]
    bf, f32 = jnp.bfloat16, jnp.float32
    vmem, smem, hbm = (pl.BlockSpec(memory_space=s) for s in (pltpu.VMEM, pltpu.SMEM, pl.ANY))
    dma = pltpu.SemaphoreType.DMA
    outs = pl.pallas_call(
        functools.partial(kernel, n_grp, n_tp),
        out_shape=(
            jax.ShapeDtypeStruct((rows, width), bf),
            jax.ShapeDtypeStruct((rows, lat), bf),
            jax.ShapeDtypeStruct((rows, rope), bf),
            jax.ShapeDtypeStruct((rows, heads, lat), bf),
        ),
        in_specs=[vmem] * 6 + [smem, vmem] + [hbm] * 7,
        out_specs=(vmem,) * 4,
        scratch_shapes=[
            pltpu.VMEM((PIECES, rows, kc + 128), bf),
            pltpu.VMEM((2, PIECES, all_rows, kc + 128), bf),
            pltpu.VMEM((2, half, ff), bf),
            pltpu.VMEM((2, half, ff), bf),
            pltpu.VMEM((2, ff, half), bf),
            pltpu.VMEM((all_rows, ff), f32),
            pltpu.VMEM((all_rows, ff), f32),
            pltpu.VMEM((all_rows, ff), bf),
            pltpu.VMEM((CHUNKS, all_rows, cw), bf),
            pltpu.VMEM((CHUNKS, all_rows, cw), bf),
            pltpu.VMEM((CHUNKS, all_rows, cw), bf),
            pltpu.VMEM((CHUNKS, n_a * rows, cw), bf),
            pltpu.VMEM((CHUNKS, n_a * rows, cw), bf),
            pltpu.VMEM((CHUNKS, n_a * rows, cw), bf),
            pltpu.VMEM((CHUNKS, n_a, rows, cw), bf),
            pltpu.VMEM((CHUNKS, rows, cw), bf),
            pltpu.VMEM((CHUNKS, rows, cw), bf),
            pltpu.VMEM((rows, lat + 128), f32),
            pltpu.VMEM((rows, lat + 128), f32),
            pltpu.VMEM(kv_proj.shape[1:], bf),
            pltpu.VMEM(cache_latent.shape[1:], bf),
            pltpu.VMEM((rows, 2 * rope, slots), bf),
            pltpu.VMEM((rows, heads, 2 * rope), bf),
            pltpu.VMEM(query_latent.shape[1:], bf),
            pltpu.VMEM((rows, heads, lat), f32),
            pltpu.VMEM((rows, heads, slots), f32),
            pltpu.VMEM((rows, heads, slots), f32),
            dma((4 * PIECES + 2,)),
            dma((PIECES, n_a)),
            dma((PIECES, n_grp)),
            dma((PIECES,)),
            dma((PIECES,)),
            dma((PIECES, n_a)),
            dma((CHUNKS,)),
            dma((CHUNKS,)),
            dma((CHUNKS,)),
            dma((CHUNKS,)),
            dma((CHUNKS, n_a)),
            dma((CHUNKS, n_a)),
            dma((CHUNKS,)),
            dma((CHUNKS,)),
            dma((2,)),
        ],
        compiler_params=pltpu.CompilerParams(
            collective_id=0, has_side_effects=True, vmem_limit_bytes=63 * 1024 * 1024
        ),
    )(
        residual[0], moe_gain, router[0], routes[0].T, attn_gain, kv_gain, lengths[0], query_rope[0],
        gate_w, up_w, down_w, kv_proj, cache_latent, cache_rope, query_latent,
    )
    final = pl.pallas_call(
        hand_over,
        out_shape=tuple(jax.ShapeDtypeStruct(o.shape, bf) for o in outs),
        in_specs=[hbm] * 4,
        out_specs=(hbm,) * 4,
        scratch_shapes=[pltpu.VMEM(o.shape, bf) for o in outs] + [dma((2, 4))],
        compiler_params=pltpu.CompilerParams(vmem_limit_bytes=63 * 1024 * 1024),
    )(*outs)
    return tuple(o[None] for o in final)


def solution(mesh):
    in_specs = (
        P("side", "grp", None),
        P("side", None),
        P("side", None, None),
        P("side", "grp", None),
        P("side", None, ("grp", "tp")),
        P("side", None, ("grp", "tp")),
        P("side", ("grp", "tp"), None),
        P("side", "tp"),
        P("side", None, "tp"),
        P("side", None),
        P("side", "grp", None, None),
        P("side", "grp", None, None),
        P("side", "grp"),
        P("side", "grp", "tp", None),
        P("side", "grp", "tp"),
    )
    out_specs = (
        P("side", "grp", None),
        P("side", "grp", None),
        P("side", "grp", None),
        P("side", "grp", "tp", None),
    )
    return jax.shard_map(body, mesh=mesh, in_specs=in_specs, out_specs=out_specs, check_vma=False)
```

```python
import functools
import math

import jax
import jax.numpy as jnp
from jax import lax
from jax.experimental import pallas as pl
from jax.experimental.pallas import tpu as pltpu
from jax.sharding import PartitionSpec as P

NORM_EPS = 1e-06
ROUTE_SCALE = 2.5
ROPE_BASE = 10000.0
SCORE_SCALE = 192.0 ** (-0.5)
MESH = pl.DeviceIdType.MESH
CHUNKS = 7
PIECES = 4
NT = (((1,), (1,)), ((), ()))


def kernel(
    n_grp, n_tp, res_ref, gain_ref, router_ref, routes_ref, again_ref, kvgain_ref, len_ref,
    qrope_ref, gate_ref, up_ref, down_ref, kvp_ref, cache_ref, crope_ref, qlat_ref,
    resid_ref, nlat_ref, nrope_ref, attn_ref,
    msg, xb, wg, wu, wd, acc_g, acc_u, hid, pown, pother, r0, sx, r1, tbuf, ra, hs, hr,
    kvs, kvr, kvw, cl, cr, qr, ql, o_acc, m_acc, l_acc,
    load_sem, d_send, d_recv, f_send, f_recv, x_send, y_send, x_recv, c_send, c_recv, z_send, z_recv, h_send, h_recv, k_sem,
):
    side = lax.axis_index("side")
    grp = lax.axis_index("grp")
    tp = lax.axis_index("tp")
    n_a = n_grp // 2
    a = grp // 2
    b = grp % 2
    rows, width = res_ref.shape
    half = width // 2
    cw = half // CHUNKS
    kc = half // PIECES
    experts = router_ref.shape[0]
    ff = gate_ref.shape[2]
    lat = kvgain_ref.shape[1]
    rope = crope_ref.shape[2]
    kvwid = lat + rope
    core_peer = (side, grp, 1 - tp)
    x_peer = (side, a * 2 + 1 - b, tp)

    def line(other_side, where):
        return (other_side, where * 2 + b, tp)

    def remote(src, dst, ssem, rsem, dev):
        return pltpu.make_async_remote_copy(
            src_ref=src, dst_ref=dst, send_sem=ssem, recv_sem=rsem, device_id=dev, device_id_type=MESH
        )

    def block(ref, which, k, pos):
        at = pl.ds(pl.multiple_of(pos * rows, rows), rows)
        return ref.at[which, k, at, :] if k == PIECES - 1 else ref.at[which, k, at, :kc]

    barrier = pltpu.get_barrier_semaphore()

    def greet():
        pl.semaphore_signal(barrier, inc=1, device_id=core_peer, device_id_type=MESH)
        for i in range(n_a):
            pl.semaphore_signal(barrier, inc=1, device_id=line(1 - side, i), device_id_type=MESH)

    @pl.when(side == 1)
    def _():
        greet()
        pl.semaphore_signal(barrier, inc=1, device_id=x_peer, device_id_type=MESH)
        own = pl.multiple_of(tp * half, 128)
        oth = pl.multiple_of((1 - tp) * half, 128)
        loads = []
        for k in range(PIECES):
            piece = pl.ds(k * kc, kc)
            for i, at in enumerate((own, oth)):
                source = pl.ds(pl.multiple_of(at + k * kc, 128), kc)
                for w_ref, w_vmem in ((gate_ref, wg), (up_ref, wu)):
                    loads.append(
                        pltpu.make_async_copy(
                            w_ref.at[0, source, :], w_vmem.at[i, piece, :], load_sem.at[len(loads)]
                        )
                    )
        for i, at in enumerate((own, oth)):
            loads.append(
                pltpu.make_async_copy(down_ref.at[0, :, pl.ds(at, half)], wd.at[i], load_sem.at[len(loads)])
            )
        for ld in loads:
            ld.start()
        pl.semaphore_wait(barrier, n_a + 2)

        sends = []

        def direct(k):
            for d in range(n_a):
                pos = b * n_a + lax.rem(a - d + n_a, n_a)
                here = block(xb, 0, k, pos)
                remote(here, here, f_send.at[k], d_recv.at[k, pos], core_peer).wait_recv()
                fwd = remote(here, here, x_send.at[k, d], d_recv.at[k, pos], x_peer)
                fwd.start()
                sends.append(fwd)

        def across(k):
            for d in range(n_a):
                pos = (1 - b) * n_a + lax.rem(a - d + n_a, n_a)
                here = block(xb, 0, k, pos)
                remote(here, here, f_send.at[k], d_recv.at[k, pos], core_peer).wait_recv()
            cp = remote(xb.at[0, k, :, :kc], xb.at[1, k, :, :kc], f_send.at[k], f_recv.at[k], core_peer)
            cp.start()
            sends.append(cp)
            return cp

        tn = min(256, ff)

        def products(k, cp):
            cp.wait_recv()
            for ld in loads[4 * k : 4 * k + 4]:
                ld.wait()
            span_k = slice(k * kc, (k + 1) * kc)

            @pl.loop(0, ff // tn)
            def _(n):
                cols = pl.ds(pl.multiple_of(n * tn, tn), tn)
                x0 = xb[0, k, :, :kc]
                x1 = xb[1, k, :, :kc]
                g = jnp.dot(x0, wg[0, span_k, cols], preferred_element_type=jnp.float32)
                g = g + jnp.dot(x1, wg[1, span_k, cols], preferred_element_type=jnp.float32)
                u = jnp.dot(x0, wu[0, span_k, cols], preferred_element_type=jnp.float32)
                u = u + jnp.dot(x1, wu[1, span_k, cols], preferred_element_type=jnp.float32)
                if k > 0:
                    g = g + acc_g[:, cols]
                    u = u + acc_u[:, cols]
                if k < PIECES - 1:
                    acc_g[:, cols] = g
                    acc_u[:, cols] = u
                else:
                    hid[:, cols] = (g / (1.0 + jnp.exp(-g)) * u).astype(jnp.bfloat16)

        direct(0)
        for k in range(1, PIECES):
            direct(k)
            products(k - 1, across(k - 1))
        products(PIECES - 1, across(PIECES - 1))

        loads[-2].wait()
        loads[-1].wait()
        span = n_grp * n_tp // experts
        expert = (grp * n_tp + tp) // span
        table = xb[0, PIECES - 1, :, kc:].astype(jnp.float32)
        lanes = lax.broadcasted_iota(jnp.int32, table.shape, 1)
        weight = jnp.sum(jnp.where(lanes == expert, table, 0.0), axis=1, keepdims=True)
        half_rows = n_a * rows
        mine = pl.ds(pl.multiple_of(b * half_rows, rows), half_rows)
        theirs = pl.ds(pl.multiple_of((1 - b) * half_rows, rows), half_rows)

        def down(j):
            h = hid[...]
            cols = slice(j * cw, (j + 1) * cw)
            p1 = jnp.dot(h, wd[1, :, cols], preferred_element_type=jnp.float32)
            pother[j] = (p1 * weight).astype(jnp.bfloat16)
            cp = remote(pother.at[j], r0.at[j], c_send.at[j], c_recv.at[j], core_peer)
            cp.start()
            p0 = jnp.dot(h, wd[0, :, cols], preferred_element_type=jnp.float32)
            pown[j] = (p0 * weight).astype(jnp.bfloat16)
            return cp

        def stage_x(j, cp):
            cp.wait_recv()
            sx[j] = (pown[j, theirs, :].astype(jnp.float32) + r0[j, theirs, :].astype(jnp.float32)).astype(jnp.bfloat16)
            xp = remote(sx.at[j], r1.at[j], y_send.at[j], x_recv.at[j], x_peer)
            xp.start()
            return xp

        def stage_z(j, xp):
            xp.wait_recv()
            tbuf[j] = (
                pown[j, mine, :].astype(jnp.float32)
                + r0[j, mine, :].astype(jnp.float32)
                + r1[j].astype(jnp.float32)
            ).astype(jnp.bfloat16)
            out = []
            for d in range(n_a):
                to_a = lax.rem(a + d, n_a)
                zp = remote(
                    tbuf.at[j, pl.ds(pl.multiple_of(to_a * rows, rows), rows), :], ra.at[j, a], z_send.at[j, d], z_recv.at[j, a], line(0, to_a)
                )
                zp.start()
                out.append(zp)
            return out

        cps, xps = [], []
        for j in range(CHUNKS):
            cps.append(down(j))
            if j >= 1:
                xps.append(stage_x(j - 1, cps[j - 1]))
        xps.append(stage_x(CHUNKS - 1, cps[-1]))
        for j in range(CHUNKS):
            sends += stage_z(j, xps[j])
        resid_ref[...] = jnp.zeros_like(resid_ref)
        nlat_ref[...] = jnp.zeros_like(nlat_ref)
        nrope_ref[...] = jnp.zeros_like(nrope_ref)
        attn_ref[...] = jnp.zeros_like(attn_ref)
        for cp in sends + cps + xps:
            cp.wait_send()

    @pl.when(side == 0)
    def _():
        loads = [
            pltpu.make_async_copy(qlat_ref.at[0], ql, load_sem.at[0]),
            pltpu.make_async_copy(cache_ref.at[0], cl, load_sem.at[1]),
            pltpu.make_async_copy(crope_ref.at[0], cr.at[:, :rope, :], load_sem.at[2]),
            pltpu.make_async_copy(crope_ref.at[0], cr.at[:, rope:, :], load_sem.at[3]),
            pltpu.make_async_copy(kvp_ref.at[0], kvw, load_sem.at[4]),
        ]
        greet()
        for ld in loads:
            ld.start()
        x = res_ref[...].astype(jnp.float32)
        scale = lax.rsqrt(jnp.mean(x * x, axis=1, keepdims=True) + NORM_EPS)
        pos = b * n_a + a
        sends = []

        def dispatch(k):
            for d in range(n_a):
                to_a = lax.rem(a + d, n_a)
                piece = msg.at[k] if k == PIECES - 1 else msg.at[k, :, :kc]
                cp = remote(piece, block(xb, 0, k, pos), d_send.at[k, d], d_recv.at[k, pos], line(1, to_a))
                cp.start()
                sends.append(cp)

        for k in range(PIECES):
            cols = pl.ds(pl.multiple_of(tp * half + k * kc, 128), kc)
            part = res_ref[:, cols].astype(jnp.float32) * scale * gain_ref[:, cols].astype(jnp.float32)
            msg[k, :, :kc] = part.astype(jnp.bfloat16)
        pl.semaphore_wait(barrier, n_a + 1)
        for k in range(PIECES - 1):
            dispatch(k)
        normed = x * scale * gain_ref[...].astype(jnp.float32)
        logits = lax.dot_general(
            router_ref[...].astype(jnp.float32), normed, NT,
            precision=lax.Precision.HIGHEST, preferred_element_type=jnp.float32,
        )
        s = 1.0 / (1.0 + jnp.exp(-logits))
        ids = lax.broadcasted_iota(jnp.int32, s.shape, 0)
        chosen = jnp.zeros(s.shape, jnp.float32)
        for k in range(routes_ref.shape[0]):
            chosen = jnp.where(routes_ref[k : k + 1, :] == ids, 1.0, chosen)
        picked = s * chosen
        dense = (ROUTE_SCALE * picked / jnp.sum(picked, axis=0, keepdims=True)).astype(jnp.bfloat16)
        eye_r = lax.broadcasted_iota(jnp.int32, (rows, rows), 0)
        eye_c = lax.broadcasted_iota(jnp.int32, (rows, rows), 1)
        eye = jnp.where(eye_r == eye_c, 1.0, 0.0).astype(jnp.bfloat16)
        dense = lax.dot_general(eye, dense, NT, preferred_element_type=jnp.float32)
        msg[PIECES - 1, :, kc:] = jnp.zeros((rows, 128), jnp.bfloat16)
        msg[PIECES - 1, :, kc : kc + experts] = dense.astype(jnp.bfloat16)
        dispatch(PIECES - 1)

        for ld in loads:
            ld.wait()

        heads = ql.shape[1]
        head_id = lax.broadcasted_iota(jnp.int32, (heads, 2 * rope), 0)
        lane_id = lax.broadcasted_iota(jnp.int32, (heads, 2 * rope), 1)
        for t in range(rows):
            fold = jnp.zeros((heads, 2 * rope), jnp.float32)
            for i in range(heads // 2):
                pair = qrope_ref[t : t + 1, i * 2 * rope : (i + 1) * 2 * rope].astype(jnp.float32)
                owner = jnp.where(lane_id < rope, 2 * i, 2 * i + 1)
                fold = jnp.where(head_id == owner, pair, fold)
            qr[t] = fold.astype(jnp.bfloat16)

        @pl.loop(0, rows)
        def _(t):
            sc = lax.dot_general(ql[t], cl[t], NT, preferred_element_type=jnp.float32)
            sc = sc + jnp.dot(qr[t], cr[t], preferred_element_type=jnp.float32)
            sc = sc * SCORE_SCALE
            usable = lax.broadcasted_iota(jnp.int32, sc.shape, 1) < len_ref[t]
            sc = jnp.where(usable, sc, -1e30)
            peak = jnp.max(sc, axis=1, keepdims=True)
            wts = jnp.where(usable, jnp.exp(sc - peak), 0.0)
            m_acc[t] = jnp.broadcast_to(peak, sc.shape)
            l_acc[t] = jnp.broadcast_to(jnp.sum(wts, axis=1, keepdims=True), sc.shape)
            o_acc[t] = jnp.dot(wts.astype(jnp.bfloat16), cl[t], preferred_element_type=jnp.float32)

        wide = (rows, 2 * rope)
        lane = lax.broadcasted_iota(jnp.int32, wide, 1)
        step = (lane % (rope // 2)).astype(jnp.float32)
        freq = jnp.exp(-(2.0 * step / rope) * math.log(ROPE_BASE))
        row_id = lax.broadcasted_iota(jnp.int32, wide, 0)
        position = jnp.zeros(wide, jnp.float32)
        for t in range(rows):
            position = jnp.where(row_id == t, len_ref[t].astype(jnp.float32), position)
        angle = position * freq
        cosine = jnp.cos(angle)
        sine = jnp.where(lane < rope // 2, -jnp.sin(angle), jnp.sin(angle))
        kv = jnp.zeros((rows, kvwid), jnp.float32)
        sq = jnp.zeros((rows, 1), jnp.float32)
        for j in range(CHUNKS):
            total = jnp.zeros((rows, cw), jnp.float32)
            for i in range(n_a):
                here = ra.at[j, i]
                remote(here, here, h_send.at[j], z_recv.at[j, i], core_peer).wait_recv()
                total = total + ra[j, i].astype(jnp.float32)
            cols = pl.ds(pl.multiple_of(tp * half + j * cw, 128), cw)
            h = (res_ref[:, cols].astype(jnp.float32) + total).astype(jnp.bfloat16)
            hs[j] = h
            cp = remote(hs.at[j], hr.at[j], h_send.at[j], h_recv.at[j], core_peer)
            cp.start()
            sends.append(cp)
            resid_ref[:, cols] = h
            hf = h.astype(jnp.float32)
            span = slice(j * cw, (j + 1) * cw)
            scaled = (hf * again_ref[:, span].astype(jnp.float32)).astype(jnp.bfloat16)
            kv = kv + lax.dot_general(scaled, kvw[:, span], NT, preferred_element_type=jnp.float32)
            sq = sq + jnp.sum(hf * hf, axis=1, keepdims=True)
        kvs[:, :kvwid] = kv
        kvs[:, kvwid:] = jnp.broadcast_to(sq, (rows, kvs.shape[1] - kvwid))
        cp = remote(kvs, kvr, k_sem.at[0], k_sem.at[1], core_peer)
        cp.start()
        sends.append(cp)
        cp.wait_recv()
        both = kvs[...] + kvr[...]
        norm = lax.rsqrt(both[:, kvwid : kvwid + 1] / width + NORM_EPS)
        latent = both[:, :lat] * norm
        lscale = lax.rsqrt(jnp.mean(latent * latent, axis=1, keepdims=True) + NORM_EPS)
        fresh = (latent * lscale * kvgain_ref[...].astype(jnp.float32)).astype(jnp.bfloat16)
        nlat_ref[...] = fresh
        rot = both[:, lat:] * norm
        up_part = pltpu.roll(rot, 128 - rope // 2, 1)
        down_part = pltpu.roll(rot, rope // 2, 1)
        turned = rot * cosine + jnp.where(lane < rope // 2, up_part, down_part) * sine
        nrope_ref[...] = turned[:, :rope].astype(jnp.bfloat16)
        turned = jnp.where(lane < rope, turned, pltpu.roll(turned, rope, 1)).astype(jnp.bfloat16)
        fresh_f = fresh.astype(jnp.float32)
        flat = rows * heads
        own = lax.dot_general(ql[...].reshape(flat, lat), fresh, NT, preferred_element_type=jnp.float32)
        own = own + lax.dot_general(
            qr[...].reshape(flat, 2 * rope), turned, NT, preferred_element_type=jnp.float32
        )
        own_row = lax.broadcasted_iota(jnp.int32, own.shape, 0) // heads
        own_col = lax.broadcasted_iota(jnp.int32, own.shape, 1)
        own = jnp.sum(jnp.where(own_row == own_col, own, 0.0), axis=1, keepdims=True) * SCORE_SCALE
        m_old = m_acc[...].reshape(flat, m_acc.shape[2])[:, :1]
        l_old = l_acc[...].reshape(flat, l_acc.shape[2])[:, :1]
        peak = jnp.maximum(m_old, own)
        keep = jnp.exp(m_old - peak)
        ow = jnp.exp(own - peak)
        inv = 1.0 / (l_old * keep + ow)
        keep = keep * inv
        ow = ow * inv
        for t in range(rows):
            at = slice(t * heads, (t + 1) * heads)
            attn_ref[t] = (o_acc[t] * keep[at] + ow[at] * fresh_f[t : t + 1]).astype(jnp.bfloat16)
        for j in range(CHUNKS):
            here = hr.at[j]
            remote(here, here, h_send.at[j], h_recv.at[j], core_peer).wait_recv()
            cols = pl.ds(pl.multiple_of((1 - tp) * half + j * cw, 128), cw)
            resid_ref[:, cols] = hr[j]
        for cp in sends:
            cp.wait_send()


def hand_over(*refs):
    ins, outs, held, sem = refs[:4], refs[4:8], refs[8:12], refs[12]
    first = [pltpu.make_async_copy(ins[i], held[i], sem.at[0, i]) for i in range(4)]
    second = [pltpu.make_async_copy(held[i], outs[i], sem.at[1, i]) for i in range(4)]
    for cp in first:
        cp.start()
    for into, out in zip(first, second):
        into.wait()
        out.start()
    for cp in second:
        cp.wait()


def body(
    residual, moe_gain, router, routes, gate_w, up_w, down_w, attn_gain, kv_proj, kv_gain,
    cache_latent, cache_rope, lengths, query_latent, query_rope,
):
    n_grp = lax.axis_size("grp")
    n_tp = lax.axis_size("tp")
    n_a = n_grp // 2
    rows, width = residual.shape[1:]
    half = width // 2
    cw = half // CHUNKS
    kc = half // PIECES
    ff = gate_w.shape[2]
    all_rows = n_grp * rows
    lat = kv_gain.shape[1]
    heads = query_latent.shape[2]
    slots = cache_latent.shape[2]
    rope = cache_rope.shape[2]
    bf, f32 = jnp.bfloat16, jnp.float32
    vmem, smem, hbm = (pl.BlockSpec(memory_space=s) for s in (pltpu.VMEM, pltpu.SMEM, pl.ANY))
    dma = pltpu.SemaphoreType.DMA
    outs = pl.pallas_call(
        functools.partial(kernel, n_grp, n_tp),
        out_shape=(
            jax.ShapeDtypeStruct((rows, width), bf),
            jax.ShapeDtypeStruct((rows, lat), bf),
            jax.ShapeDtypeStruct((rows, rope), bf),
            jax.ShapeDtypeStruct((rows, heads, lat), bf),
        ),
        in_specs=[vmem] * 6 + [smem, vmem] + [hbm] * 7,
        out_specs=(vmem,) * 4,
        scratch_shapes=[
            pltpu.VMEM((PIECES, rows, kc + 128), bf),
            pltpu.VMEM((2, PIECES, all_rows, kc + 128), bf),
            pltpu.VMEM((2, half, ff), bf),
            pltpu.VMEM((2, half, ff), bf),
            pltpu.VMEM((2, ff, half), bf),
            pltpu.VMEM((all_rows, ff), f32),
            pltpu.VMEM((all_rows, ff), f32),
            pltpu.VMEM((all_rows, ff), bf),
            pltpu.VMEM((CHUNKS, all_rows, cw), bf),
            pltpu.VMEM((CHUNKS, all_rows, cw), bf),
            pltpu.VMEM((CHUNKS, all_rows, cw), bf),
            pltpu.VMEM((CHUNKS, n_a * rows, cw), bf),
            pltpu.VMEM((CHUNKS, n_a * rows, cw), bf),
            pltpu.VMEM((CHUNKS, n_a * rows, cw), bf),
            pltpu.VMEM((CHUNKS, n_a, rows, cw), bf),
            pltpu.VMEM((CHUNKS, rows, cw), bf),
            pltpu.VMEM((CHUNKS, rows, cw), bf),
            pltpu.VMEM((rows, lat + 128), f32),
            pltpu.VMEM((rows, lat + 128), f32),
            pltpu.VMEM(kv_proj.shape[1:], bf),
            pltpu.VMEM(cache_latent.shape[1:], bf),
            pltpu.VMEM((rows, 2 * rope, slots), bf),
            pltpu.VMEM((rows, heads, 2 * rope), bf),
            pltpu.VMEM(query_latent.shape[1:], bf),
            pltpu.VMEM((rows, heads, lat), f32),
            pltpu.VMEM((rows, heads, slots), f32),
            pltpu.VMEM((rows, heads, slots), f32),
            dma((4 * PIECES + 2,)),
            dma((PIECES, n_a)),
            dma((PIECES, n_grp)),
            dma((PIECES,)),
            dma((PIECES,)),
            dma((PIECES, n_a)),
            dma((CHUNKS,)),
            dma((CHUNKS,)),
            dma((CHUNKS,)),
            dma((CHUNKS,)),
            dma((CHUNKS, n_a)),
            dma((CHUNKS, n_a)),
            dma((CHUNKS,)),
            dma((CHUNKS,)),
            dma((2,)),
        ],
        compiler_params=pltpu.CompilerParams(
            collective_id=0, has_side_effects=True, vmem_limit_bytes=63 * 1024 * 1024
        ),
    )(
        residual[0], moe_gain, router[0], routes[0].T, attn_gain, kv_gain, lengths[0], query_rope[0],
        gate_w, up_w, down_w, kv_proj, cache_latent, cache_rope, query_latent,
    )
    final = pl.pallas_call(
        hand_over,
        out_shape=tuple(jax.ShapeDtypeStruct(o.shape, bf) for o in outs),
        in_specs=[hbm] * 4,
        out_specs=(hbm,) * 4,
        scratch_shapes=[pltpu.VMEM(o.shape, bf) for o in outs] + [dma((2, 4))],
        compiler_params=pltpu.CompilerParams(vmem_limit_bytes=63 * 1024 * 1024),
    )(*outs)
    return tuple(o[None] for o in final)


def solution(mesh):
    in_specs = (
        P("side", "grp", None),
        P("side", None),
        P("side", None, None),
        P("side", "grp", None),
        P("side", None, ("grp", "tp")),
        P("side", None, ("grp", "tp")),
        P("side", ("grp", "tp"), None),
        P("side", "tp"),
        P("side", None, "tp"),
        P("side", None),
        P("side", "grp", None, None),
        P("side", "grp", None, None),
        P("side", "grp"),
        P("side", "grp", "tp", None),
        P("side", "grp", "tp"),
    )
    out_specs = (
        P("side", "grp", None),
        P("side", "grp", None),
        P("side", "grp", None),
        P("side", "grp", "tp", None),
    )
    return jax.shard_map(body, mesh=mesh, in_specs=in_specs, out_specs=out_specs, check_vma=False)
```
